256 devices in a mesh: grp: 8 (over y, core), blk: 32 (over z, x).
Axes of the slice: x: 4, y: 4, z: 8, core: 2. Of those that a mesh axis runs over, the one named last changes fastest.
Arguments:
- rhs: float32 [12288, 1920], P(('grp', 'blk')), may hold values from -6 to 6
- membership: int32 [12288], P(('grp', 'blk')), may hold values from 0 to 7
- pair_ends: int32 [131072, 2], P(('grp', 'blk')), may hold values from 0 to 63, as said below
- pair_dir: int32 [131072], P(('grp', 'blk')), may hold values from 0 to 2
- pair_reach: float32 [131072], P(('grp', 'blk')), may hold values from 0.05 to 0.25
- pair_count: int32 [256], P(('grp', 'blk')), may hold values from 256 to 512, as said below
- send_idx: int32 [256, 14, 4], P(('grp', 'blk')), may hold values from 0 to 7
- rotation: float32 [3, 15, 128, 128], replicated, may hold values from -0.5 to 0.5
- translation: float32 [15, 128, 128], replicated, may hold values from -0.5 to 0.5
- mie: float32 [1920], replicated, may hold values from 0.2 to 1
Outputs:
- basis: float32 [12288, 1920], P(('grp', 'blk'))
- image: float32 [12288, 1920], P(('grp', 'blk'))
The draws below stay inside these ranges and needn't reach their ends.
Inputs may be any that keep to these rules, and one draw needn't show every extreme that they name: `pair_ends`: column 0 names a cluster of the pair's own device. Column 1 names either another cluster of the same device (below 8, never equal to column 0) or 8 + k * 4 + slot, the cluster sent in that slot by the neighbour at offset k, and only neighbours that lie on the grid are named. Every row of a neighbour on the grid is named by some pair among the first 256 pair slots of its device. `pair_count`: some device has all 512 pair slots live.
All inputs are finite; a program needn't handle non-finite values.
Results may differ from the reference program's by a relative error of at most 0.000053.
Values sent between devices are 32-bit elements; how exact they have to be, the bound alone decides.
No kernel may reach another device: no remote copies, remote signals or barrier semaphores. Data moves between devices by JAX's collectives and lax.ppermute only.
A program may use at most 128 MiB of HBM per device.

```python
import math
import jax
import jax.numpy as jnp
from jax import lax

C = 1920
BK = 128
NB = 15
NDIR = 3
NPEER = 14
K_DEV = 8
P_DEV = 512
CAP = 4
S_DEV = 48
GROUPS = 8
BLOCKS = 32
NDEV = 256
ROWS_IN = 56
HALF_P = 256


def draw_pair_ends(key, part):
    base = jax.random.fold_in(key, 11)

    def one_device(index):
        device_key = jax.random.fold_in(base, index)
        key_place, key_first, key_other, key_local = jax.random.split(device_key, 4)
        device_row = index // BLOCKS
        device_col = index % BLOCKS
        offsets = jnp.arange(NPEER, dtype=jnp.int32)
        offset_f = offsets + (offsets >= 7).astype(jnp.int32)
        source_row = device_row - (offset_f // 5 - 1)
        source_col = device_col - (offset_f % 5 - 2)
        valid = (source_row >= 0) & (source_row < GROUPS) & (source_col >= 0) & (source_col < BLOCKS)
        row_valid = valid[jnp.arange(ROWS_IN, dtype=jnp.int32) // CAP]
        place = jax.random.permutation(key_place, HALF_P).astype(jnp.int32)
        ranks = jnp.zeros((HALF_P,), jnp.int32).at[place].set(jnp.arange(HALF_P, dtype=jnp.int32))
        ranks = jnp.concatenate([ranks, jnp.full((P_DEV - HALF_P,), HALF_P, jnp.int32)])
        first = jax.random.randint(key_first, (P_DEV,), 0, K_DEV, dtype=jnp.int32)
        other = jax.random.randint(key_other, (P_DEV,), 0, K_DEV + ROWS_IN - 1, dtype=jnp.int32)
        other = other + (other >= first).astype(jnp.int32)
        second = jnp.where(ranks < ROWS_IN, K_DEV + ranks, other)
        remote_pos = jnp.clip(second - K_DEV, 0, ROWS_IN - 1)
        usable = (second < K_DEV) | row_valid[remote_pos]
        step_local = jax.random.randint(key_local, (P_DEV,), 1, K_DEV, dtype=jnp.int32)
        fallback = (first + step_local) % K_DEV
        second = jnp.where(usable, second, fallback)
        return jnp.stack([first, second], axis=1)
    table = jax.vmap(one_device)(jnp.arange(NDEV, dtype=jnp.int32))
    return table.reshape(NDEV * P_DEV, 2)


def draw_pair_count(key, part):
    base = jax.random.fold_in(key, 23)
    key_counts, key_where = jax.random.split(base)
    counts = jax.random.randint(key_counts, (NDEV,), HALF_P, P_DEV + 1, dtype=jnp.int32)
    where = jax.random.randint(key_where, (), 0, NDEV, dtype=jnp.int32)
    return counts.at[where].set(P_DEV)


def with_ends(values, stream_key, smallest, top_value):
    index_at = [jax.random.randint(jax.random.fold_in(stream_key, axis), (), 0, length) for axis, length in enumerate(values.shape)]
    main_axis = values.shape.index(max(values.shape))
    next_to = index_at[:main_axis] + [(index_at[main_axis] + 1) % values.shape[main_axis]] + index_at[main_axis + 1:]
    return values.at[tuple(index_at)].set(smallest).at[tuple(next_to)].set(top_value)


def level_of(stream_key, extent, cuts, smallest, largest):
    def one(dim, parts):
        steps = jax.random.uniform(jax.random.fold_in(jax.random.fold_in(stream_key, 6), dim), (parts,), jnp.float32, smallest / len(cuts), largest / len(cuts))
        return jnp.repeat(jnp.exp(steps), extent[dim] // parts).reshape((-1,) + (1,) * (len(extent) - dim - 1))

    level = one(*cuts[0])
    for cut in cuts[1:]:
        level = level * one(*cut)
    return level


def gaussian(rng, extent, spread, reach, shards=(), kind=jnp.bfloat16):
    loudness = level_of(rng, extent, shards, -0.22, 0.18) if shards else 1.0
    values = jax.random.normal(rng, extent, jnp.float32) * spread * loudness
    return jnp.minimum(jnp.maximum(values, -reach), reach).astype(kind)


def setup_inputs(seed: int = 0) -> dict:
    key_list = jax.random.split(jax.random.key(seed), 11)
    rhs = gaussian(key_list[0], (NDEV * S_DEV, C), 1.0, 6.0, ((0, 256),), jnp.float32)
    membership = with_ends(jax.random.randint(key_list[1], (NDEV * S_DEV,), 0, K_DEV), jax.random.fold_in(key_list[1], 1), 0, K_DEV - 1).astype(jnp.int32)
    pair_ends = draw_pair_ends(jax.random.fold_in(key_list[10], 71), 0)
    pair_dir = with_ends(jax.random.randint(key_list[3], (NDEV * P_DEV,), 0, NDIR), jax.random.fold_in(key_list[3], 1), 0, NDIR - 1).astype(jnp.int32)
    pair_reach = jnp.clip(jnp.exp(math.log(0.25) - 1.609438 * jax.random.uniform(key_list[4], (NDEV * P_DEV,), jnp.float32) ** level_of(key_list[4], (NDEV * P_DEV,), ((0, 256),), -0.2, 0.2)), 0.05, 0.25)
    pair_count = draw_pair_count(jax.random.fold_in(key_list[10], 71), 0)
    send_idx = with_ends(jax.random.randint(key_list[6], (NDEV, NPEER, CAP), 0, K_DEV), jax.random.fold_in(key_list[6], 1), 0, K_DEV - 1).astype(jnp.int32)
    rotation = gaussian(key_list[7], (NDIR, NB, BK, BK), BK ** -0.5, 0.5, (), jnp.float32)
    translation = gaussian(key_list[8], (NB, BK, BK), BK ** -0.5, 0.5, (), jnp.float32)
    mie = jnp.clip(jax.random.uniform(key_list[9], (C,), jnp.float32, 0.2, 1.0), 0.2, 1.0)
    return dict(rhs=rhs, membership=membership, pair_ends=pair_ends, pair_dir=pair_dir, pair_reach=pair_reach, pair_count=pair_count, send_idx=send_idx, rotation=rotation, translation=translation, mie=mie)


HI = lax.Precision.HIGHEST

def rotate_rows(rows, rotation):
    count = rows.shape[0]
    split = rows.reshape(count, NB, BK)
    out = jnp.einsum('mgk,dgkj->mdgj', split, rotation, precision=HI)
    return out.reshape(count, NDIR, C)

def translate_frames(front, behind, translation):
    count = front.shape[0]
    half = BK // 2
    first_part = jnp.roll(front, half, axis=2).reshape(count, NDIR, NB, BK)
    second_part = jnp.roll(behind, half, axis=2).reshape(count, NDIR, NB, BK)
    out = jnp.einsum('mdgk,gkj->mdgj', first_part, translation, precision=HI)
    out = out + jnp.einsum('mdgk,gjk->mdgj', second_part, translation, precision=HI)
    return jnp.roll(out.reshape(count, NDIR, C), -half, axis=2)

def unrotate_frames(frames, rotation):
    count = frames.shape[0]
    split = frames.reshape(count, NDIR, NB, BK)
    out = jnp.einsum('mdgj,dgkj->mgk', split, rotation, precision=HI)
    return out.reshape(count, C)

def reference(rhs, membership, pair_ends, pair_dir, pair_reach, pair_count, send_idx, rotation, translation, mie):
    clusters_all = NDEV * K_DEV
    sphere_dev = (jnp.arange(NDEV * S_DEV, dtype=jnp.int32) // S_DEV).astype(jnp.int32)
    cluster_id = (sphere_dev * K_DEV + membership).astype(jnp.int32)
    pair_owner = (jnp.arange(NDEV * P_DEV, dtype=jnp.int32) // P_DEV).astype(jnp.int32)
    position = (jnp.arange(NDEV * P_DEV, dtype=jnp.int32) % P_DEV).astype(jnp.int32)
    first_end = (pair_owner * K_DEV + pair_ends[:, 0]).astype(jnp.int32)
    second = pair_ends[:, 1]
    remote_row = jnp.clip(second - K_DEV, 0, ROWS_IN - 1).astype(jnp.int32)
    offset_k = (remote_row // CAP).astype(jnp.int32)
    slot = (remote_row % CAP).astype(jnp.int32)
    offset_f = (offset_k + (offset_k >= 7).astype(jnp.int32)).astype(jnp.int32)
    row_shift = (offset_f // 5 - 1).astype(jnp.int32)
    col_shift = (offset_f % 5 - 2).astype(jnp.int32)
    owner_row = (pair_owner // BLOCKS).astype(jnp.int32)
    owner_col = (pair_owner % BLOCKS).astype(jnp.int32)
    source_row = jnp.clip(owner_row - row_shift, 0, GROUPS - 1).astype(jnp.int32)
    source_col = jnp.clip(owner_col - col_shift, 0, BLOCKS - 1).astype(jnp.int32)
    source = (source_row * BLOCKS + source_col).astype(jnp.int32)
    sent = send_idx.reshape(-1)[((source * NPEER + offset_k) * CAP + slot).astype(jnp.int32)]
    second_end = jnp.where(second >= K_DEV, source * K_DEV + sent, pair_owner * K_DEV + second).astype(jnp.int32)
    live = (position < pair_count[pair_owner]).astype(jnp.float32)
    weight = pair_reach * live
    own_index = (first_end * NDIR + pair_dir).astype(jnp.int32)
    near_index = (second_end * NDIR + pair_dir).astype(jnp.int32)

    def operator(vector):
        gathered = jax.ops.segment_sum(vector, cluster_id, num_segments=clusters_all)
        frames = rotate_rows(gathered, rotation).reshape(clusters_all * NDIR, C)
        front = jax.ops.segment_sum(weight[:, None] * frames[near_index], own_index, num_segments=clusters_all * NDIR)
        behind = jax.ops.segment_sum(weight[:, None] * frames[own_index], near_index, num_segments=clusters_all * NDIR)
        moved = translate_frames(front.reshape(clusters_all, NDIR, C), behind.reshape(clusters_all, NDIR, C), translation)
        field = unrotate_frames(moved, rotation)
        return vector - mie[None, :] * field[cluster_id]
    entries = float(NDEV * S_DEV * C)
    scale = jnp.sqrt(jnp.sum(rhs * rhs) / entries + 1e-06)
    start = rhs / scale
    first_image = operator(start)
    proj = jnp.sum(start * first_image) / entries
    rest = first_image - proj * start
    norm = jnp.sqrt(jnp.sum(rest * rest) / entries + 1e-06)
    basis = rest / norm
    return (basis, operator(basis))
```

```python
import functools

import jax
import jax.numpy as jnp
from jax import lax
from jax.experimental import pallas as pl
from jax.experimental.pallas import tpu as pltpu
from jax.sharding import Mesh
from jax.sharding import PartitionSpec as P

F32 = jnp.float32
BF16 = jnp.bfloat16
HI = lax.Precision.HIGHEST
ALL = ("y", "c", "z", "x")
ROW = ("z", "x")
COL = ("y", "c")
K = 8
C = 1920
NB = 15
W = 128
NPEER = 14
CAP = 4
EXTRA = 256
VMEM_LIMIT = 24 * 1024 * 1024

NN = (((1,), (0,)), ((), ()))
NT = (((1,), (1,)), ((), ()))
TN = (((0,), (0,)), ((), ()))


def dot(a, b, dims=NN):
    return lax.dot_general(a, b, dims, precision=HI, preferred_element_type=F32)


def halves(x):
    high = x.astype(BF16)
    return high, (x - high.astype(F32)).astype(BF16)


def dot3(a, b, dims=NN):
    rows = a.shape[0]
    a_high32 = a.astype(BF16).astype(F32)
    both = jnp.concatenate([a_high32, a - a_high32], axis=0).astype(BF16)
    b_high, b_low = halves(b)
    first = lax.dot_general(both, b_high, dims, preferred_element_type=F32)
    second = lax.dot_general(a.astype(BF16), b_low, dims, preferred_element_type=F32)
    return first[:rows] + first[rows:] + second


def lanes(shape):
    return lax.broadcasted_iota(jnp.int32, shape, 1)


def sublanes(shape):
    return lax.broadcasted_iota(jnp.int32, shape, 0)


def gather_kernel(count_ref, rhs_ref, member_ref, ends_ref, dir_ref, reach_ref, send_ref, out_ref, square_ref, pad_ref):
    spheres = rhs_ref.shape[0]
    pairs = dir_ref.shape[1]
    rhs = rhs_ref[...]
    member = (sublanes((K, spheres)) == member_ref[...]).astype(F32)
    out_ref[:, :C] = dot(member, rhs)
    squares = jnp.sum(rhs * rhs, axis=0, keepdims=True)
    partial = squares[:, :W]
    for g in range(1, NB):
        partial = partial + squares[:, g * W : (g + 1) * W]
    square_ref[...] = partial
    weight = jnp.where(lanes((1, pairs)) < count_ref[0], reach_ref[...], 0.0)
    own = ends_ref[0:1, :]
    near = ends_ref[1:2, :]
    far = near - K
    place = jnp.where(near < K, near, K + NPEER * (far & (CAP - 1)) + (far >> 2))
    rows = sublanes((W, pairs)) & 63
    near_hot = (rows == place).astype(F32)
    own_weight = jnp.where(sublanes((K, pairs)) == own, weight, 0.0)
    lane = lanes((K, W))
    blocks = [dot(jnp.where(dir_ref[...] == d, own_weight, 0.0), near_hot, NT) for d in range(3)]
    pad_ref[...] = jnp.zeros_like(pad_ref)
    pad_ref[0:CAP, 0:NPEER] = send_ref[...].astype(F32)
    names = jnp.where(lane < 64 + K, (lane - 64).astype(F32), 0.0)
    for slot in range(CAP):
        row = jnp.broadcast_to(pad_ref[slot : slot + 1, :], (K, W))
        names = names + pltpu.roll(row, 64 + K + NPEER * slot, 1)
    out_ref[:, C : C + W] = jnp.where(lane < 64, blocks[0], blocks[1])
    out_ref[:, C + W :] = jnp.where(lane < 64, blocks[2], names)


def pair_matrix(units):
    x = lax.axis_index("x")
    c = lax.axis_index("c")
    core = 1 - 2 * c
    one = 1 - 2 * (x & 1)
    two = jnp.where(x < 2, 2, -2)
    lane = lanes((K, W))
    low = lane < 64
    half = lane & 63
    seen = half - K
    peer = seen - NPEER * (
        (seen >= NPEER).astype(jnp.int32)
        + (seen >= 2 * NPEER).astype(jnp.int32)
        + (seen >= 3 * NPEER).astype(jnp.int32)
    )
    peer = jnp.where(half < K, -1, peer)
    names_of = sublanes((K, W)).astype(F32)
    hot, first, second = [], [], []
    for group, d_row in enumerate((0, core, -core)):
        for place, d_col in enumerate((0, one, -one, two, -two)):
            v0, v1 = units[group * 5 + place]
            names = jnp.where(low, pltpu.roll(v1, 64, 1), v1)
            if group == 0 and place == 0:
                here = peer == -1
                there = here
                own_hot = jnp.where(names == names_of, 1.0, 0.0)
            else:
                f = (1 - d_row) * 5 + 2 - d_col
                b = 14 - f
                here = peer == f - (f > 7).astype(jnp.int32)
                there = peer == b - (b > 7).astype(jnp.int32)
            hot.append(jnp.where((names == names_of) & here, 1.0, 0.0))
            first.append(jnp.where(there, v0, 0.0))
            second.append(jnp.where(there & low, v1, 0.0))
    hot = jnp.concatenate(hot, axis=0)
    first = jnp.concatenate(first, axis=0)
    second = jnp.concatenate(second, axis=0)
    v0, v1 = units[0]

    def two_classes(v):
        return jnp.concatenate([jnp.where(low, v, 0.0), jnp.where(low, 0.0, v)], axis=0)

    return jnp.concatenate(
        [
            dot(two_classes(v0), hot, NT),
            dot(jnp.where(low, v1, 0.0), hot, NT),
            dot(two_classes(own_hot), first, NT),
            dot(jnp.where(low, own_hot, 0.0), second, NT),
        ],
        axis=0,
    )


def field_of(matrix, rows, rotation_ref, translation_ref, y_ref, z_ref):
    ends = dot3(matrix, rows)
    low = lanes((3 * K, W)) < 64
    for g in range(NB):
        at = slice(g * W, (g + 1) * W)
        for d in range(3):
            pair = jnp.concatenate([ends[d * K : d * K + K, at], ends[24 + d * K : 24 + d * K + K, at]], axis=0)
            turned = pltpu.roll(dot3(pair, rotation_ref[d, g]), 64, 1)
            y_ref[d * K : d * K + K, at] = turned[:K]
            y_ref[24 + d * K : 24 + d * K + K, at] = turned[K:]
    for g in range(NB):
        at = slice(g * W, (g + 1) * W)
        b = (g - 1) % NB
        before = slice(b * W, (b + 1) * W)
        front = jnp.where(low, y_ref[:24, before], y_ref[:24, at])
        behind = jnp.where(low, y_ref[24:, before], y_ref[24:, at])
        moved = dot3(front, translation_ref[g]) + dot3(behind, translation_ref[g], NT)
        z_ref[:, at] = pltpu.roll(moved, 64, 1)
    out = []
    for g in range(NB):
        at = slice(g * W, (g + 1) * W)
        a = (g + 1) % NB
        z = jnp.where(low, z_ref[:, at], z_ref[:, a * W : (a + 1) * W])
        out.append(sum(dot3(z[d * K : d * K + K], rotation_ref[d, g], NT) for d in range(3)))
    return out


def first_kernel(
    own_ref, core_ref, side_ref, member_ref, square_ref, rotation_ref, translation_ref, mie_ref,
    matrix_ref, field_ref, next_ref, sums_ref, y_ref, z_ref,
):
    refs = [r.at[i] for r in (own_ref, core_ref, side_ref) for i in range(5)]
    matrix = pair_matrix([(r[:, C : C + W], r[:, C + W : C + 2 * W]) for r in refs])
    matrix_ref[...] = matrix
    rows = jnp.concatenate([r[:, :C] for r in refs], axis=0)
    field = field_of(matrix, rows, rotation_ref, translation_ref, y_ref, z_ref)
    spheres = member_ref.shape[1]
    member = (sublanes((K, spheres)) == member_ref[...]).astype(F32)
    count = jnp.sum(member, axis=1, keepdims=True)
    inner = jnp.zeros((K, W), F32)
    square = jnp.zeros((K, W), F32)
    for g in range(NB):
        at = slice(g * W, (g + 1) * W)
        scaled = field[g] * mie_ref[:, at]
        total = scaled * count
        field_ref[:, at] = scaled
        next_ref[:, at] = total
        inner = inner + scaled * own_ref[0, :, at]
        square = square + scaled * total
    sums_ref[...] = jnp.zeros_like(sums_ref)
    sums_ref[0:1, :] = square_ref[...]
    sums_ref[1:2, :] = jnp.sum(inner, axis=0, keepdims=True)
    sums_ref[2:3, :] = jnp.sum(square, axis=0, keepdims=True)


def second_kernel(
    own_ref, core_ref, side_ref, matrix_ref, rotation_ref, translation_ref, mie_ref, field_ref, y_ref, z_ref
):
    rows = jnp.concatenate([r[i] for r in (own_ref, core_ref, side_ref) for i in range(5)], axis=0)
    field = field_of(matrix_ref[...], rows, rotation_ref, translation_ref, y_ref, z_ref)
    for g in range(NB):
        at = slice(g * W, (g + 1) * W)
        field_ref[:, at] = field[g] * mie_ref[:, at]


def last_kernel(entries, rhs_ref, member_ref, first_ref, second_ref, sums_ref, basis_ref, image_ref):
    sums = jnp.sum(sums_ref[...], axis=1, keepdims=True) / entries
    s, t, u = sums[0:1], sums[1:2], sums[2:3]
    scale2 = s + 1e-06
    rest = (1e-06 + t) / scale2
    norm = jnp.sqrt((rest * rest * s - 2.0 * rest * t + u) / scale2 + 1e-06)
    factor = 1.0 / (norm * jnp.sqrt(scale2))
    spheres = rhs_ref.shape[0]
    member = (sublanes((K, spheres)) == member_ref[...]).astype(F32)
    first = first_ref[...] * factor
    change = rest * first - second_ref[...] * factor
    basis = (rest * factor) * rhs_ref[...] - dot(member, first, TN)
    basis_ref[...] = basis
    image_ref[...] = basis - dot(member, change, TN)


def call(kernel, out_shape, scratch=(), smem=0, inputs=0):
    space = [pl.BlockSpec(memory_space=pltpu.SMEM)] * smem + [pl.BlockSpec(memory_space=pltpu.VMEM)] * (inputs - smem)
    return pl.pallas_call(
        kernel,
        out_shape=out_shape,
        in_specs=space,
        scratch_shapes=list(scratch),
        compiler_params=pltpu.CompilerParams(vmem_limit_bytes=VMEM_LIMIT),
    )


def like(*shape):
    return jax.ShapeDtypeStruct(shape, F32)


def swap(v, axis, mask):
    return lax.ppermute(v, axis, [(i, i ^ mask) for i in range(lax.axis_size(axis))])


def spread(v):
    length = lax.axis_size("z")
    x = lax.axis_index("x")
    near = swap(v, "x", 1)
    pair = jnp.stack([v, near])
    far = swap(pair, "x", 3)
    hops = [(z * 4 + i, (z + 1) * 4 + i) for z in range(length - 1) for i in (0, 1)]
    hops += [(z * 4 + i, (z - 1) * 4 + i) for z in range(1, length) for i in (2, 3)]
    deep = lax.ppermute(far, ROW, hops)
    edge = (x == 0) | (x == 3)
    line = jnp.stack([v, near, jnp.where(edge, deep[0], far[0]), far[1], deep[1]])
    other = swap(line, "c", 1)
    last = lax.axis_size("y") * 2 - 1
    steps = [(i, i + 1) for i in range(1, last, 2)] + [(i + 1, i) for i in range(1, last, 2)]
    side = lax.ppermute(line, COL, steps)
    return line, other, side


def total(v):
    for axis, masks in (("x", (1, 3)), ("c", (1,)), ("y", (1, 3)), ("z", (1, 2, 4))):
        for mask in masks:
            v = v + swap(v, axis, mask)
    return v


def body(rhs, membership, pair_ends, pair_dir, pair_reach, pair_count, send_idx, rotation, translation, mie):
    spheres = rhs.shape[0]
    pairs = pair_dir.shape[0]
    member = membership.reshape(1, spheres)
    mie = mie.reshape(1, C)
    packed, squares = call(
        gather_kernel, (like(K, C + EXTRA), like(1, W)), [pltpu.VMEM((K, W), F32)], smem=1, inputs=7
    )(
        pair_count,
        rhs,
        member,
        pair_ends.T,
        pair_dir.reshape(1, pairs),
        pair_reach.reshape(1, pairs),
        jnp.transpose(send_idx, (0, 2, 1)).reshape(CAP, NPEER),
    )
    work = [pltpu.VMEM((6 * K, C), F32), pltpu.VMEM((3 * K, C), F32)]
    matrix, first, following, sums = call(
        first_kernel, (like(6 * K, 15 * K), like(K, C), like(K, C), like(K, W)), work, inputs=8
    )(*spread(packed), member, squares, rotation, translation, mie)
    second = call(second_kernel, like(K, C), work, inputs=7)(*spread(following), matrix, rotation, translation, mie)
    sums = total(sums)
    entries = float(lax.axis_size(ALL) * spheres * C)
    return tuple(
        call(functools.partial(last_kernel, entries), (like(spheres, C), like(spheres, C)), inputs=5)(
            rhs, member, first, second, sums
        )
    )


def solution(mesh):
    torus = Mesh(mesh.devices.reshape(4, 2, 8, 4), ALL)
    return jax.shard_map(
        body,
        mesh=torus,
        in_specs=(
            P(ALL, None),
            P(ALL),
            P(ALL, None),
            P(ALL),
            P(ALL),
            P(ALL),
            P(ALL, None, None),
            P(),
            P(),
            P(),
        ),
        out_specs=(P(ALL, None), P(ALL, None)),
        check_vma=False,
    )
```

```python
import functools

import jax
import jax.numpy as jnp
from jax import lax
from jax.experimental import pallas as pl
from jax.experimental.pallas import tpu as pltpu
from jax.sharding import Mesh
from jax.sharding import PartitionSpec as P

F32 = jnp.float32
BF16 = jnp.bfloat16
HI = lax.Precision.HIGHEST
ALL = ("y", "c", "z", "x")
ROW = ("z", "x")
COL = ("y", "c")
K = 8
C = 1920
NB = 15
W = 128
NPEER = 14
CAP = 4
EXTRA = 256
VMEM_LIMIT = 24 * 1024 * 1024

NN = (((1,), (0,)), ((), ()))
NT = (((1,), (1,)), ((), ()))
TN = (((0,), (0,)), ((), ()))


def dot(a, b, dims=NN):
    return lax.dot_general(a, b, dims, precision=HI, preferred_element_type=F32)


def halves(x):
    high = x.astype(BF16)
    return high, (x - high.astype(F32)).astype(BF16)


def dot3(a, b, dims=NN):
    rows = a.shape[0]
    a_high32 = a.astype(BF16).astype(F32)
    both = jnp.concatenate([a_high32, a - a_high32], axis=0).astype(BF16)
    b_high, b_low = halves(b)
    first = lax.dot_general(both, b_high, dims, preferred_element_type=F32)
    second = lax.dot_general(a.astype(BF16), b_low, dims, preferred_element_type=F32)
    return first[:rows] + first[rows:] + second


def lanes(shape):
    return lax.broadcasted_iota(jnp.int32, shape, 1)


def sublanes(shape):
    return lax.broadcasted_iota(jnp.int32, shape, 0)


def gather_kernel(count_ref, *refs):
    sources, (out_ref, square_ref, rhs_ref), (pad_ref, member_ref, ends_ref, dir_ref, reach_ref, send_ref, sem) = (
        refs[:6],
        refs[6:9],
        refs[9:],
    )
    targets = (rhs_ref, member_ref, ends_ref, dir_ref, reach_ref, send_ref)
    copies = [pltpu.make_async_copy(a, b, sem.at[i]) for i, (a, b) in enumerate(zip(sources, targets))]
    for copy in copies:
        copy.start()
    for copy in copies:
        copy.wait()
    spheres = rhs_ref.shape[0]
    pairs = dir_ref.shape[1]
    rhs = rhs_ref[...]
    member = (sublanes((K, spheres)) == member_ref[...]).astype(F32)
    out_ref[:, :C] = dot(member, rhs)
    squares = jnp.sum(rhs * rhs, axis=0, keepdims=True)
    partial = squares[:, :W]
    for g in range(1, NB):
        partial = partial + squares[:, g * W : (g + 1) * W]
    square_ref[...] = partial
    weight = jnp.where(lanes((1, pairs)) < count_ref[0], reach_ref[...], 0.0)
    own = ends_ref[0:1, :]
    near = ends_ref[1:2, :]
    far = near - K
    place = jnp.where(near < K, near, K + NPEER * (far & (CAP - 1)) + (far >> 2))
    rows = sublanes((W, pairs)) & 63
    near_hot = (rows == place).astype(F32)
    own_weight = jnp.where(sublanes((K, pairs)) == own, weight, 0.0)
    lane = lanes((K, W))
    blocks = [dot(jnp.where(dir_ref[...] == d, own_weight, 0.0), near_hot, NT) for d in range(3)]
    pad_ref[...] = jnp.zeros_like(pad_ref)
    pad_ref[0:CAP, 0:NPEER] = send_ref[...].astype(F32)
    names = jnp.where(lane < 64 + K, (lane - 64).astype(F32), 0.0)
    for slot in range(CAP):
        row = jnp.broadcast_to(pad_ref[slot : slot + 1, :], (K, W))
        names = names + pltpu.roll(row, 64 + K + NPEER * slot, 1)
    out_ref[:, C : C + W] = jnp.where(lane < 64, blocks[0], blocks[1])
    out_ref[:, C + W :] = jnp.where(lane < 64, blocks[2], names)


def pair_matrix(units):
    x = lax.axis_index("x")
    c = lax.axis_index("c")
    core = 1 - 2 * c
    one = 1 - 2 * (x & 1)
    two = jnp.where(x < 2, 2, -2)
    lane = lanes((K, W))
    low = lane < 64
    half = lane & 63
    seen = half - K
    peer = seen - NPEER * (
        (seen >= NPEER).astype(jnp.int32)
        + (seen >= 2 * NPEER).astype(jnp.int32)
        + (seen >= 3 * NPEER).astype(jnp.int32)
    )
    peer = jnp.where(half < K, -1, peer)
    names_of = sublanes((K, W)).astype(F32)
    hot, first, second = [], [], []
    for group, d_row in enumerate((0, core, -core)):
        for place, d_col in enumerate((0, one, -one, two, -two)):
            v0, v1 = units[group * 5 + place]
            names = jnp.where(low, pltpu.roll(v1, 64, 1), v1)
            if group == 0 and place == 0:
                here = peer == -1
                there = here
                own_hot = jnp.where(names == names_of, 1.0, 0.0)
            else:
                f = (1 - d_row) * 5 + 2 - d_col
                b = 14 - f
                here = peer == f - (f > 7).astype(jnp.int32)
                there = peer == b - (b > 7).astype(jnp.int32)
            hot.append(jnp.where((names == names_of) & here, 1.0, 0.0))
            first.append(jnp.where(there, v0, 0.0))
            second.append(jnp.where(there & low, v1, 0.0))
    hot = jnp.concatenate(hot, axis=0)
    first = jnp.concatenate(first, axis=0)
    second = jnp.concatenate(second, axis=0)
    v0, v1 = units[0]

    def two_classes(v):
        return jnp.concatenate([jnp.where(low, v, 0.0), jnp.where(low, 0.0, v)], axis=0)

    return jnp.concatenate(
        [
            dot(two_classes(v0), hot, NT),
            dot(jnp.where(low, v1, 0.0), hot, NT),
            dot(two_classes(own_hot), first, NT),
            dot(jnp.where(low, own_hot, 0.0), second, NT),
        ],
        axis=0,
    )


def stacked(x):
    high = x.astype(BF16).astype(F32)
    return jnp.concatenate([high, x - high], axis=0).astype(BF16)


def times(x, parts):
    rows, columns = x.shape[0], parts.shape[1] // 2
    out = lax.dot_general(stacked(x), parts, NN, preferred_element_type=F32)
    return out[:rows, :columns] + (out[:rows, columns:] + out[rows:, :columns]) + out[rows:, columns:]


def split_kernel(rotation_any, translation_any, turn_ref, move_ref, back_ref, rotation_ref, translation_ref, sem):
    copies = start_all((rotation_any, translation_any), (rotation_ref, translation_ref), sem)

    def put(ref, g, row, w):
        ref[g, row : row + W, :] = jnp.concatenate(halves(w), axis=1)

    copies[0].wait()
    for g in range(NB):
        for d in range(3):
            w = rotation_ref[d, g]
            put(turn_ref, g, d * W, w)
            put(back_ref, g, d * W, w.T)
    copies[1].wait()
    for g in range(NB):
        w = translation_ref[g]
        put(move_ref, g, 0, w)
        put(move_ref, g, W, w.T)


def field_of(matrix, rows, turn_ref, move_ref, back_ref):
    ends = dot3(matrix, rows)
    low = lanes((3 * K, W)) < 64
    turned = []
    for g in range(NB):
        at = slice(g * W, (g + 1) * W)
        parts = []
        for d in range(3):
            pair = jnp.concatenate([ends[d * K : d * K + K, at], ends[24 + d * K : 24 + d * K + K, at]], axis=0)
            parts.append(pltpu.roll(times(pair, turn_ref[g, d * W : (d + 1) * W, :]), 64, 1))
        front = jnp.concatenate([p[:K] for p in parts], axis=0)
        behind = jnp.concatenate([p[K:] for p in parts], axis=0)
        turned.append((front, behind))
    moved = []
    for g in range(NB):
        both = [jnp.where(low, before, here) for before, here in zip(turned[g - 1], turned[g])]
        moved.append(pltpu.roll(times(jnp.concatenate(both, axis=1), move_ref[g]), 64, 1))
    out = []
    for g in range(NB):
        z = jnp.where(low, moved[g], moved[(g + 1) % NB])
        flat = jnp.concatenate([z[d * K : d * K + K] for d in range(3)], axis=1)
        out.append(times(flat, back_ref[g]))
    return out


def start_all(sources, targets, sem):
    copies = [pltpu.make_async_copy(a, b, sem.at[i]) for i, (a, b) in enumerate(zip(sources, targets))]
    for copy in copies:
        copy.start()
    return copies


def first_kernel(
    own_ref, core_ref, side_ref, square_ref, turn_ref, move_ref, back_ref, mie_ref, member_ref,
    matrix_ref, field_ref, next_ref,
):
    refs = [r.at[i] for r in (own_ref, core_ref, side_ref) for i in range(5)]
    matrix = pair_matrix([(r[:, C : C + W], r[:, C + W : C + 2 * W]) for r in refs])
    matrix_ref[...] = matrix
    rows = jnp.concatenate([r[:, :C] for r in refs], axis=0)
    field = field_of(matrix, rows, turn_ref, move_ref, back_ref)
    spheres = member_ref.shape[1]
    member = (sublanes((K, spheres)) == member_ref[...]).astype(F32)
    count = jnp.sum(member, axis=1, keepdims=True)
    inner = jnp.zeros((K, W), F32)
    square = jnp.zeros((K, W), F32)
    for g in range(NB):
        at = slice(g * W, (g + 1) * W)
        scaled = field[g] * mie_ref[g : g + 1, :]
        total = scaled * count
        field_ref[:, at] = scaled
        next_ref[:, at] = total
        inner = inner + scaled * own_ref[0, :, at]
        square = square + scaled * total
    row = sublanes((K, W))
    inner = jnp.sum(inner, axis=0, keepdims=True)
    square = jnp.sum(square, axis=0, keepdims=True)
    next_ref[:, C:] = jnp.where(row == 0, square_ref[...], jnp.where(row == 1, inner, jnp.where(row == 2, square, 0.0)))


def second_kernel(own_ref, core_ref, side_ref, matrix_ref, turn_ref, move_ref, back_ref, mie_ref, field_ref):
    rows = jnp.concatenate([r[i] for r in (own_ref, core_ref, side_ref) for i in range(5)], axis=0)
    field = field_of(matrix_ref[...], rows, turn_ref, move_ref, back_ref)
    for g in range(NB):
        at = slice(g * W, (g + 1) * W)
        field_ref[:, at] = field[g] * mie_ref[g : g + 1, :]


def last_kernel(entries, rhs_ref, member_ref, first_ref, second_ref, sums_ref, basis_ref, image_ref):
    sums = jnp.sum(sums_ref[...], axis=1, keepdims=True) / entries
    s, t, u = sums[0:1], sums[1:2], sums[2:3]
    scale2 = s + 1e-06
    rest = (1e-06 + t) / scale2
    norm = jnp.sqrt((rest * rest * s - 2.0 * rest * t + u) / scale2 + 1e-06)
    factor = 1.0 / (norm * jnp.sqrt(scale2))
    spheres = rhs_ref.shape[0]
    member = (sublanes((K, spheres)) == member_ref[...]).astype(F32)
    first = first_ref[...] * factor
    change = rest * first - second_ref[...] * factor
    basis = (rest * factor) * rhs_ref[...] - dot(member, first, TN)
    basis_ref[...] = basis
    image_ref[...] = basis - dot(member, change, TN)


def call(kernel, out_shape, vmem, anywhere=0, scratch=(), smem=0, work=0):
    space = [pl.BlockSpec(memory_space=pltpu.SMEM)] * smem + [pl.BlockSpec(memory_space=pltpu.VMEM)] * vmem
    space += [pl.BlockSpec(memory_space=pltpu.HBM)] * anywhere
    run = pl.pallas_call(
        kernel,
        out_shape=out_shape,
        in_specs=space,
        scratch_shapes=list(scratch),
        compiler_params=pltpu.CompilerParams(vmem_limit_bytes=VMEM_LIMIT),
        cost_estimate=pl.CostEstimate(flops=work, bytes_accessed=0, transcendentals=0) if work else None,
    )

    def placed(*operands):
        held = [pltpu.with_memory_space_constraint(v, pltpu.HBM) for v in operands[smem + vmem :]]
        return run(*operands[: smem + vmem], *held)

    return placed


def like(*shape):
    return jax.ShapeDtypeStruct(shape, F32)


def swap(v, axis, mask):
    return lax.ppermute(v, axis, [(i, i ^ mask) for i in range(lax.axis_size(axis))])


def beside(v):
    length = lax.axis_size("z")
    inside = [(4 * z + 1, 4 * z + 2) for z in range(length)]
    devices = 4 * length
    odd = inside + [(4 * z + 3, (4 * z + 4) % devices) for z in range(length)]
    wide = [(4 * z + i, (4 * z + i + 2) % devices) for z in range(length) for i in (2, 3)]
    return (
        swap(v, "x", 1),
        lax.ppermute(v, ROW, odd + [(b, a) for a, b in odd]),
        swap(v, "x", 2),
        lax.ppermute(v, ROW, wide + [(b, a) for a, b in wide]),
    )


def across(line):
    devices = lax.axis_size(COL)
    steps = [(i, (i + 1) % devices) for i in range(1, devices, 2)]
    side = lax.ppermute(line, COL, steps + [(b, a) for a, b in steps])
    return line, swap(line, "c", 1), side


def plus(v, axis, masks):
    return functools.reduce(jnp.add, [v] + [swap(v, axis, mask) for mask in masks])


def body(rhs, membership, pair_ends, pair_dir, pair_reach, pair_count, send_idx, rotation, translation, mie):
    spheres = rhs.shape[0]
    pairs = pair_dir.shape[0]
    member = membership.reshape(1, spheres)
    mie = mie.reshape(NB, W)
    whole = [
        pltpu.VMEM((1, spheres), jnp.int32),
        pltpu.VMEM((2, pairs), jnp.int32),
        pltpu.VMEM((1, pairs), jnp.int32),
        pltpu.VMEM((1, pairs), F32),
        pltpu.VMEM((CAP, NPEER), jnp.int32),
        pltpu.SemaphoreType.DMA((6,)),
    ]
    packed, squares, kept = call(
        gather_kernel,
        (like(K, C + EXTRA), like(1, W), like(spheres, C)),
        0,
        6,
        [pltpu.VMEM((K, W), F32)] + whole,
        1,
    )(
        pair_count,
        rhs,
        member,
        pair_ends.T,
        pair_dir.reshape(1, pairs),
        pair_reach.reshape(1, pairs),
        jnp.transpose(send_idx, (0, 2, 1)).reshape(CAP, NPEER),
    )
    weights = call(
        split_kernel,
        tuple(jax.ShapeDtypeStruct((NB, rows * W, 2 * W), BF16) for rows in (3, 2, 3)),
        0,
        2,
        [pltpu.VMEM(rotation.shape, F32), pltpu.VMEM(translation.shape, F32), pltpu.SemaphoreType.DMA((2,))],
        work=3 * 10**9,
    )(rotation, translation)
    line = jnp.stack((packed,) + beside(packed))
    matrix, first, following = call(first_kernel, (like(6 * K, 15 * K), like(K, C), like(K, C + W)), 9)(
        *across(line), squares, *weights, mie, member
    )
    near = beside(following)
    line = jnp.stack([v[:, :C] for v in (following,) + near])
    own = following[:, C:]
    sums = own + near[0][:, C:] + near[2][:, C:] + swap(own, "x", 3)
    around = across(line)
    sums = plus(sums, "z", (4, 2, 6))
    second = call(second_kernel, like(K, C), 8, work=5 * 10**9)(*around, matrix, *weights, mie)
    sums = plus(sums, "y", (2, 1, 3))
    sums = plus(plus(sums, "c", (1,)), "z", (1,))
    entries = float(lax.axis_size(ALL) * spheres * C)
    return tuple(
        call(functools.partial(last_kernel, entries), (like(spheres, C), like(spheres, C)), 5)(
            kept, member, first, second, sums
        )
    )


def solution(mesh):
    torus = Mesh(mesh.devices.reshape(4, 2, 8, 4), ALL)
    return jax.shard_map(
        body,
        mesh=torus,
        in_specs=(
            P(ALL, None),
            P(ALL),
            P(ALL, None),
            P(ALL),
            P(ALL),
            P(ALL),
            P(ALL, None, None),
            P(),
            P(),
            P(),
        ),
        out_specs=(P(ALL, None), P(ALL, None)),
        check_vma=False,
    )
```

```python
import functools

import jax
import jax.numpy as jnp
from jax import lax
from jax.experimental import pallas as pl
from jax.experimental.pallas import tpu as pltpu
from jax.sharding import Mesh
from jax.sharding import PartitionSpec as P

F32 = jnp.float32
BF16 = jnp.bfloat16
ALL = ("y", "c", "z", "x")
ROW = ("z", "x")
COL = ("y", "c")
K = 8
C = 1920
NB = 15
W = 128
NPEER = 14
CAP = 4
EXTRA = 256
VMEM_LIMIT = 24 * 1024 * 1024

NN = (((1,), (0,)), ((), ()))
NT = (((1,), (1,)), ((), ()))
TN = (((0,), (0,)), ((), ()))


def halves(x):
    high = x.astype(BF16)
    return high, (x - high.astype(F32)).astype(BF16)


def dot3(a, b, dims=NN):
    rows = a.shape[0]
    a_high32 = a.astype(BF16).astype(F32)
    both = jnp.concatenate([a_high32, a - a_high32], axis=0).astype(BF16)
    b_high, b_low = halves(b)
    first = lax.dot_general(both, b_high, dims, preferred_element_type=F32)
    second = lax.dot_general(a.astype(BF16), b_low, dims, preferred_element_type=F32)
    return first[:rows] + first[rows:] + second


def thirds(x):
    high = x.astype(BF16).astype(F32)
    rest = x - high
    middle = rest.astype(BF16).astype(F32)
    return high, middle, rest - middle


def weighted_hot(x, hot):
    rows = x.shape[0]
    out = lax.dot_general(
        jnp.concatenate(thirds(x), axis=0).astype(BF16), hot.astype(BF16), NT, preferred_element_type=F32
    )
    return out[:rows] + out[rows : 2 * rows] + out[2 * rows :]


def hot_times(hot, x, dims=NN):
    hot = hot.astype(BF16)
    return sum(lax.dot_general(hot, part.astype(BF16), dims, preferred_element_type=F32) for part in thirds(x))


def rows_of(member, x):
    return lax.dot_general(
        jnp.concatenate([member] * 3, axis=0).astype(BF16),
        jnp.concatenate(thirds(x), axis=0).astype(BF16),
        TN,
        preferred_element_type=F32,
    )


def lanes(shape):
    return lax.broadcasted_iota(jnp.int32, shape, 1)


def sublanes(shape):
    return lax.broadcasted_iota(jnp.int32, shape, 0)


def gather_kernel(count_ref, *refs):
    sources, (out_ref, square_ref, rhs_ref), (pad_ref, member_ref, ends_ref, dir_ref, reach_ref, send_ref, sem) = (
        refs[:6],
        refs[6:9],
        refs[9:],
    )
    targets = (rhs_ref, member_ref, ends_ref, dir_ref, reach_ref, send_ref)
    copies = [pltpu.make_async_copy(a, b, sem.at[i]) for i, (a, b) in enumerate(zip(sources, targets))]
    for copy in copies:
        copy.start()
    for copy in copies:
        copy.wait()
    spheres = rhs_ref.shape[0]
    pairs = dir_ref.shape[1]
    rhs = rhs_ref[...]
    member = (sublanes((K, spheres)) == member_ref[...]).astype(F32)
    out_ref[:, :C] = hot_times(member, rhs)
    squares = jnp.sum(rhs * rhs, axis=0, keepdims=True)
    partial = squares[:, :W]
    for g in range(1, NB):
        partial = partial + squares[:, g * W : (g + 1) * W]
    square_ref[...] = partial
    weight = jnp.where(lanes((1, pairs)) < count_ref[0], reach_ref[...], 0.0)
    own = ends_ref[0:1, :]
    near = ends_ref[1:2, :]
    far = near - K
    place = jnp.where(near < K, near, K + NPEER * (far & (CAP - 1)) + (far >> 2))
    rows = sublanes((W, pairs)) & 63
    near_hot = (rows == place).astype(F32)
    own_weight = jnp.where(sublanes((K, pairs)) == own, weight, 0.0)
    lane = lanes((K, W))
    classes = jnp.concatenate([jnp.where(dir_ref[...] == d, own_weight, 0.0) for d in range(3)], axis=0)
    table = weighted_hot(classes, near_hot)
    blocks = [table[d * K : d * K + K] for d in range(3)]
    pad_ref[...] = jnp.zeros_like(pad_ref)
    pad_ref[0:CAP, 0:NPEER] = send_ref[...].astype(F32)
    names = jnp.where(lane < 64 + K, (lane - 64).astype(F32), 0.0)
    for slot in range(CAP):
        row = jnp.broadcast_to(pad_ref[slot : slot + 1, :], (K, W))
        names = names + pltpu.roll(row, 64 + K + NPEER * slot, 1)
    out_ref[:, C : C + W] = jnp.where(lane < 64, blocks[0], blocks[1])
    out_ref[:, C + W :] = jnp.where(lane < 64, blocks[2], names)


def pair_matrix(units):
    x = lax.axis_index("x")
    c = lax.axis_index("c")
    core = 1 - 2 * c
    one = 1 - 2 * (x & 1)
    two = jnp.where(x < 2, 2, -2)
    lane = lanes((K, W))
    low = lane < 64
    half = lane & 63
    seen = half - K
    peer = seen - NPEER * (
        (seen >= NPEER).astype(jnp.int32)
        + (seen >= 2 * NPEER).astype(jnp.int32)
        + (seen >= 3 * NPEER).astype(jnp.int32)
    )
    peer = jnp.where(half < K, -1, peer)
    names_of = sublanes((K, W)).astype(F32)
    hot, first, second = [], [], []
    for group, d_row in enumerate((0, core, -core)):
        for place, d_col in enumerate((0, one, -one, two, -two)):
            v0, v1 = units[group * 5 + place]
            names = jnp.where(low, pltpu.roll(v1, 64, 1), v1)
            if group == 0 and place == 0:
                here = peer == -1
                there = here
                own_hot = jnp.where(names == names_of, 1.0, 0.0)
            else:
                f = (1 - d_row) * 5 + 2 - d_col
                b = 14 - f
                here = peer == f - (f > 7).astype(jnp.int32)
                there = peer == b - (b > 7).astype(jnp.int32)
            hot.append(jnp.where((names == names_of) & here, 1.0, 0.0))
            first.append(jnp.where(there, v0, 0.0))
            second.append(jnp.where(there & low, v1, 0.0))
    hot = jnp.concatenate(hot, axis=0)
    first = jnp.concatenate(first, axis=0)
    second = jnp.concatenate(second, axis=0)
    v0, v1 = units[0]

    def two_classes(v):
        return jnp.concatenate([jnp.where(low, v, 0.0), jnp.where(low, 0.0, v)], axis=0)

    ends = jnp.concatenate([two_classes(v0), jnp.where(low, v1, 0.0)], axis=0)
    return jnp.concatenate(
        [
            weighted_hot(ends, hot),
            hot_times(two_classes(own_hot), first, NT),
            hot_times(jnp.where(low, own_hot, 0.0), second, NT),
        ],
        axis=0,
    )


def stacked(x):
    high = x.astype(BF16).astype(F32)
    return jnp.concatenate([high, x - high], axis=0).astype(BF16)


def times(x, parts):
    rows, columns = x.shape[0], parts.shape[1] // 2
    out = lax.dot_general(stacked(x), parts, NN, preferred_element_type=F32)
    return out[:rows, :columns] + (out[:rows, columns:] + out[rows:, :columns]) + out[rows:, columns:]


def split_kernel(rotation_any, translation_any, turn_ref, move_ref, back_ref, rotation_ref, translation_ref, sem):
    copies = start_all((rotation_any, translation_any), (rotation_ref, translation_ref), sem)

    def put(ref, g, row, w):
        ref[g, row : row + W, :] = jnp.concatenate(halves(w), axis=1)

    copies[0].wait()
    for g in range(NB):
        for d in range(3):
            w = rotation_ref[d, g]
            put(turn_ref, g, d * W, w)
            put(back_ref, g, d * W, w.T)
    copies[1].wait()
    for g in range(NB):
        w = translation_ref[g]
        put(move_ref, g, 0, w)
        put(move_ref, g, W, w.T)


def field_of(matrix, rows, turn_ref, move_ref, back_ref):
    ends = dot3(matrix, rows)
    low = lanes((3 * K, W)) < 64
    turned = []
    for g in range(NB):
        at = slice(g * W, (g + 1) * W)
        parts = []
        for d in range(3):
            pair = jnp.concatenate([ends[d * K : d * K + K, at], ends[24 + d * K : 24 + d * K + K, at]], axis=0)
            parts.append(pltpu.roll(times(pair, turn_ref[g, d * W : (d + 1) * W, :]), 64, 1))
        front = jnp.concatenate([p[:K] for p in parts], axis=0)
        behind = jnp.concatenate([p[K:] for p in parts], axis=0)
        turned.append((front, behind))
    moved = []
    for g in range(NB):
        both = [jnp.where(low, before, here) for before, here in zip(turned[g - 1], turned[g])]
        moved.append(pltpu.roll(times(jnp.concatenate(both, axis=1), move_ref[g]), 64, 1))
    out = []
    for g in range(NB):
        z = jnp.where(low, moved[g], moved[(g + 1) % NB])
        flat = jnp.concatenate([z[d * K : d * K + K] for d in range(3)], axis=1)
        out.append(times(flat, back_ref[g]))
    return out


def start_all(sources, targets, sem):
    copies = [pltpu.make_async_copy(a, b, sem.at[i]) for i, (a, b) in enumerate(zip(sources, targets))]
    for copy in copies:
        copy.start()
    return copies


def first_kernel(
    own_ref, core_ref, side_ref, square_ref, turn_ref, move_ref, back_ref, mie_ref, member_ref,
    matrix_ref, field_ref, next_ref,
):
    refs = [r.at[i] for r in (own_ref, core_ref, side_ref) for i in range(5)]
    matrix = pair_matrix([(r[:, C : C + W], r[:, C + W : C + 2 * W]) for r in refs])
    matrix_ref[...] = matrix
    rows = jnp.concatenate([r[:, :C] for r in refs], axis=0)
    field = field_of(matrix, rows, turn_ref, move_ref, back_ref)
    spheres = member_ref.shape[1]
    member = (sublanes((K, spheres)) == member_ref[...]).astype(F32)
    count = jnp.sum(member, axis=1, keepdims=True)
    inner = jnp.zeros((K, W), F32)
    square = jnp.zeros((K, W), F32)
    for g in range(NB):
        at = slice(g * W, (g + 1) * W)
        scaled = field[g] * mie_ref[g : g + 1, :]
        total = scaled * count
        field_ref[:, at] = scaled
        next_ref[:, at] = total
        inner = inner + scaled * own_ref[0, :, at]
        square = square + scaled * total
    row = sublanes((K, W))
    inner = jnp.sum(inner, axis=0, keepdims=True)
    square = jnp.sum(square, axis=0, keepdims=True)
    next_ref[:, C:] = jnp.where(row == 0, square_ref[...], jnp.where(row == 1, inner, jnp.where(row == 2, square, 0.0)))


def second_kernel(
    own_ref, core_ref, side_ref, matrix_ref, turn_ref, move_ref, back_ref, mie_ref, member_ref, first_ref,
    near_ref, next_ref,
):
    core = [core_ref[i * K : i * K + K, :] for i in range(5)]
    rows = jnp.concatenate([own_ref[i] for i in range(5)] + core + [side_ref[i] for i in range(5)], axis=0)
    field = field_of(matrix_ref[...], rows, turn_ref, move_ref, back_ref)
    spheres = member_ref.shape[1]
    member = (sublanes((K, spheres)) == member_ref[...]).astype(F32)
    for g in range(NB):
        at = slice(g * W, (g + 1) * W)
        near_ref[:, at] = rows_of(member, first_ref[:, at])
        next_ref[:, at] = rows_of(member, field[g] * mie_ref[g : g + 1, :])


def last_kernel(entries, rhs_ref, first_ref, second_ref, sums_ref, basis_ref, image_ref):
    sums = jnp.sum(sums_ref[...], axis=1, keepdims=True) / entries
    s, t, u = sums[0:1], sums[1:2], sums[2:3]
    scale2 = s + 1e-06
    rest = (1e-06 + t) / scale2
    norm = jnp.sqrt((rest * rest * s - 2.0 * rest * t + u) / scale2 + 1e-06)
    factor = 1.0 / (norm * jnp.sqrt(scale2))
    first = first_ref[...] * factor
    basis = (rest * factor) * rhs_ref[...] - first
    basis_ref[...] = basis
    image_ref[...] = basis - (rest * first - second_ref[...] * factor)


def call(kernel, out_shape, vmem, anywhere=0, scratch=(), smem=0, work=0):
    space = [pl.BlockSpec(memory_space=pltpu.SMEM)] * smem + [pl.BlockSpec(memory_space=pltpu.VMEM)] * vmem
    space += [pl.BlockSpec(memory_space=pltpu.HBM)] * anywhere
    run = pl.pallas_call(
        kernel,
        out_shape=out_shape,
        in_specs=space,
        scratch_shapes=list(scratch),
        compiler_params=pltpu.CompilerParams(vmem_limit_bytes=VMEM_LIMIT),
        cost_estimate=pl.CostEstimate(flops=work, bytes_accessed=0, transcendentals=0) if work else None,
    )

    def placed(*operands):
        held = [pltpu.with_memory_space_constraint(v, pltpu.HBM) for v in operands[smem + vmem :]]
        return run(*operands[: smem + vmem], *held)

    return placed


def like(*shape):
    return jax.ShapeDtypeStruct(shape, F32)


def swap(v, axis, mask):
    return lax.ppermute(v, axis, [(i, i ^ mask) for i in range(lax.axis_size(axis))])


def beside(v):
    length = lax.axis_size("z")
    inside = [(4 * z + 1, 4 * z + 2) for z in range(length)]
    devices = 4 * length
    odd = inside + [(4 * z + 3, (4 * z + 4) % devices) for z in range(length)]
    wide = [(4 * z + i, (4 * z + i + 2) % devices) for z in range(length) for i in (2, 3)]
    return (
        swap(v, "x", 1),
        lax.ppermute(v, ROW, odd + [(b, a) for a, b in odd]),
        swap(v, "x", 2),
        lax.ppermute(v, ROW, wide + [(b, a) for a, b in wide]),
    )


def over_side(line):
    devices = lax.axis_size(COL)
    steps = [(i, (i + 1) % devices) for i in range(1, devices, 2)]
    return lax.ppermute(line, COL, steps + [(b, a) for a, b in steps])


def after(v, other):
    return lax.optimization_barrier((v, other))[0]


def plus(v, axis, masks):
    return functools.reduce(jnp.add, [v] + [swap(v, axis, mask) for mask in masks])


def body(rhs, membership, pair_ends, pair_dir, pair_reach, pair_count, send_idx, rotation, translation, mie):
    spheres = rhs.shape[0]
    pairs = pair_dir.shape[0]
    member = membership.reshape(1, spheres)
    mie = mie.reshape(NB, W)
    whole = [
        pltpu.VMEM((1, spheres), jnp.int32),
        pltpu.VMEM((2, pairs), jnp.int32),
        pltpu.VMEM((1, pairs), jnp.int32),
        pltpu.VMEM((1, pairs), F32),
        pltpu.VMEM((CAP, NPEER), jnp.int32),
        pltpu.SemaphoreType.DMA((6,)),
    ]
    packed, squares, kept = call(
        gather_kernel,
        (like(K, C + EXTRA), like(1, W), like(spheres, C)),
        0,
        6,
        [pltpu.VMEM((K, W), F32)] + whole,
        1,
    )(
        pair_count,
        rhs,
        member,
        pair_ends.T,
        pair_dir.reshape(1, pairs),
        pair_reach.reshape(1, pairs),
        jnp.transpose(send_idx, (0, 2, 1)).reshape(CAP, NPEER),
    )
    weights = call(
        split_kernel,
        tuple(jax.ShapeDtypeStruct((NB, rows * W, 2 * W), BF16) for rows in (3, 2, 3)),
        0,
        2,
        [pltpu.VMEM(rotation.shape, F32), pltpu.VMEM(translation.shape, F32), pltpu.SemaphoreType.DMA((2,))],
        work=3 * 10**9,
    )(rotation, translation)
    line = jnp.stack((packed,) + beside(packed))
    matrix, first, following = call(first_kernel, (like(6 * K, 15 * K), like(K, C), like(K, C + W)), 9)(
        line, swap(line, "c", 1), over_side(line), squares, *weights, mie, member
    )
    near = beside(following)
    line = jnp.stack([v[:, :C] for v in (following,) + near])
    sums = after(sum(v[:, C:] for v in near[:3]) + following[:, C:], near[3])
    carried = jnp.concatenate([line.reshape(5 * K, C), jnp.pad(sums, ((0, 0), (0, C - W)))], axis=0)
    core = swap(carried, "c", 1)
    side = over_side(line)
    sums = sums + core[5 * K :, :W]
    near, second = call(second_kernel, (like(spheres, C), like(spheres, C)), 10, work=5 * 10**9)(
        line, core, side, matrix, *weights, mie, member, first
    )
    sums = plus(sums, "z", (2, 6, 4))
    sums = plus(sums, "y", (2, 1, 3))
    sums = plus(after(sums, second), "z", (1,))
    entries = float(lax.axis_size(ALL) * spheres * C)
    return tuple(
        call(functools.partial(last_kernel, entries), (like(spheres, C), like(spheres, C)), 4)(
            kept, near, second, sums
        )
    )


def solution(mesh):
    torus = Mesh(mesh.devices.reshape(4, 2, 8, 4), ALL)
    return jax.shard_map(
        body,
        mesh=torus,
        in_specs=(
            P(ALL, None),
            P(ALL),
            P(ALL, None),
            P(ALL),
            P(ALL),
            P(ALL),
            P(ALL, None, None),
            P(),
            P(),
            P(),
        ),
        out_specs=(P(ALL, None), P(ALL, None)),
        check_vma=False,
    )
```

```python
import functools

import jax
import jax.numpy as jnp
from jax import lax
from jax.experimental import pallas as pl
from jax.experimental.pallas import tpu as pltpu
from jax.sharding import Mesh
from jax.sharding import PartitionSpec as P

F32 = jnp.float32
BF16 = jnp.bfloat16
ALL = ("y", "c", "z", "x")
ROW = ("z", "x")
COL = ("y", "c")
K = 8
C = 1920
NB = 15
W = 128
NPEER = 14
CAP = 4
EXTRA = 256
VMEM_LIMIT = 24 * 1024 * 1024

NN = (((1,), (0,)), ((), ()))
NT = (((1,), (1,)), ((), ()))
TN = (((0,), (0,)), ((), ()))


def halves(x):
    high = x.astype(BF16)
    return high, (x - high.astype(F32)).astype(BF16)


def dot3(a, b, dims=NN):
    rows = a.shape[0]
    a_high32 = a.astype(BF16).astype(F32)
    both = jnp.concatenate([a_high32, a - a_high32], axis=0).astype(BF16)
    b_high, b_low = halves(b)
    first = lax.dot_general(both, b_high, dims, preferred_element_type=F32)
    second = lax.dot_general(a.astype(BF16), b_low, dims, preferred_element_type=F32)
    return first[:rows] + first[rows:] + second


def thirds(x):
    high = x.astype(BF16).astype(F32)
    rest = x - high
    middle = rest.astype(BF16).astype(F32)
    return high, middle, rest - middle


def weighted_hot(x, hot):
    rows = x.shape[0]
    out = lax.dot_general(
        jnp.concatenate(thirds(x), axis=0).astype(BF16), hot.astype(BF16), NT, preferred_element_type=F32
    )
    return out[:rows] + out[rows : 2 * rows] + out[2 * rows :]


def hot_times(hot, x, dims=NN):
    hot = hot.astype(BF16)
    return sum(lax.dot_general(hot, part.astype(BF16), dims, preferred_element_type=F32) for part in thirds(x))


def rows_of(member, x):
    return lax.dot_general(
        jnp.concatenate([member] * 3, axis=0).astype(BF16),
        jnp.concatenate(thirds(x), axis=0).astype(BF16),
        TN,
        preferred_element_type=F32,
    )


def lanes(shape):
    return lax.broadcasted_iota(jnp.int32, shape, 1)


def sublanes(shape):
    return lax.broadcasted_iota(jnp.int32, shape, 0)


def gather_kernel(count_ref, *refs):
    sources, (out_ref, square_ref, rhs_ref), (pad_ref, member_ref, ends_ref, dir_ref, reach_ref, send_ref, sem) = (
        refs[:6],
        refs[6:9],
        refs[9:],
    )
    targets = (rhs_ref, member_ref, ends_ref, dir_ref, reach_ref, send_ref)
    copies = [pltpu.make_async_copy(a, b, sem.at[i]) for i, (a, b) in enumerate(zip(sources, targets))]
    for copy in copies:
        copy.start()
    for copy in copies:
        copy.wait()
    spheres = rhs_ref.shape[0]
    pairs = dir_ref.shape[1]
    rhs = rhs_ref[...]
    member = (sublanes((K, spheres)) == member_ref[...]).astype(F32)
    out_ref[:, :C] = hot_times(member, rhs)
    squares = jnp.sum(rhs * rhs, axis=0, keepdims=True)
    partial = squares[:, :W]
    for g in range(1, NB):
        partial = partial + squares[:, g * W : (g + 1) * W]
    square_ref[...] = partial
    weight = jnp.where(lanes((1, pairs)) < count_ref[0], reach_ref[...], 0.0)
    own = ends_ref[0:1, :]
    near = ends_ref[1:2, :]
    far = near - K
    place = jnp.where(near < K, near, K + NPEER * (far & (CAP - 1)) + (far >> 2))
    rows = sublanes((W, pairs)) & 63
    near_hot = (rows == place).astype(F32)
    own_weight = jnp.where(sublanes((K, pairs)) == own, weight, 0.0)
    lane = lanes((K, W))
    classes = jnp.concatenate([jnp.where(dir_ref[...] == d, own_weight, 0.0) for d in range(3)], axis=0)
    table = weighted_hot(classes, near_hot)
    blocks = [table[d * K : d * K + K] for d in range(3)]
    pad_ref[...] = jnp.zeros_like(pad_ref)
    pad_ref[0:CAP, 0:NPEER] = send_ref[...].astype(F32)
    names = jnp.where(lane < 64 + K, (lane - 64).astype(F32), 0.0)
    for slot in range(CAP):
        row = jnp.broadcast_to(pad_ref[slot : slot + 1, :], (K, W))
        names = names + pltpu.roll(row, 64 + K + NPEER * slot, 1)
    out_ref[:, C : C + W] = jnp.where(lane < 64, blocks[0], blocks[1])
    out_ref[:, C + W :] = jnp.where(lane < 64, blocks[2], names)


def pair_matrix(units):
    x = lax.axis_index("x")
    c = lax.axis_index("c")
    core = 1 - 2 * c
    one = 1 - 2 * (x & 1)
    two = jnp.where(x < 2, 2, -2)
    lane = lanes((K, W))
    low = lane < 64
    half = lane & 63
    seen = half - K
    peer = seen - NPEER * (
        (seen >= NPEER).astype(jnp.int32)
        + (seen >= 2 * NPEER).astype(jnp.int32)
        + (seen >= 3 * NPEER).astype(jnp.int32)
    )
    peer = jnp.where(half < K, -1, peer)
    names_of = sublanes((K, W)).astype(F32)
    hot, first, second = [], [], []
    for group, d_row in enumerate((0, core, -core)):
        for place, d_col in enumerate((0, one, -one, two, -two)):
            v0, v1 = units[group * 5 + place]
            names = jnp.where(low, pltpu.roll(v1, 64, 1), v1)
            if group == 0 and place == 0:
                here = peer == -1
                there = here
                own_hot = jnp.where(names == names_of, 1.0, 0.0)
            else:
                f = (1 - d_row) * 5 + 2 - d_col
                b = 14 - f
                here = peer == f - (f > 7).astype(jnp.int32)
                there = peer == b - (b > 7).astype(jnp.int32)
            hot.append(jnp.where((names == names_of) & here, 1.0, 0.0))
            first.append(jnp.where(there, v0, 0.0))
            second.append(jnp.where(there & low, v1, 0.0))
    hot = jnp.concatenate(hot, axis=0)
    first = jnp.concatenate(first, axis=0)
    second = jnp.concatenate(second, axis=0)
    v0, v1 = units[0]

    def two_classes(v):
        return jnp.concatenate([jnp.where(low, v, 0.0), jnp.where(low, 0.0, v)], axis=0)

    ends = jnp.concatenate([two_classes(v0), jnp.where(low, v1, 0.0)], axis=0)
    return jnp.concatenate(
        [
            weighted_hot(ends, hot),
            hot_times(two_classes(own_hot), first, NT),
            hot_times(jnp.where(low, own_hot, 0.0), second, NT),
        ],
        axis=0,
    )


def stacked(x):
    high = x.astype(BF16).astype(F32)
    return jnp.concatenate([high, x - high], axis=0).astype(BF16)


def times(x, parts):
    rows, columns = x.shape[0], parts.shape[1] // 2
    out = lax.dot_general(stacked(x), parts, NN, preferred_element_type=F32)
    return out[:rows, :columns] + (out[:rows, columns:] + out[rows:, :columns]) + out[rows:, columns:]


def split_kernel(rotation_any, translation_any, turn_ref, move_ref, back_ref, rotation_ref, translation_ref, sem):
    copies = start_all((rotation_any, translation_any), (rotation_ref, translation_ref), sem)

    def put(ref, g, row, w):
        ref[g, row : row + W, :] = jnp.concatenate(halves(w), axis=1)

    copies[0].wait()
    for g in range(NB):
        for d in range(3):
            w = rotation_ref[d, g]
            put(turn_ref, g, d * W, w)
            put(back_ref, g, d * W, w.T)
    copies[1].wait()
    for g in range(NB):
        w = translation_ref[g]
        put(move_ref, g, 0, w)
        put(move_ref, g, W, w.T)


def field_of(matrix, rows, turn_ref, move_ref, back_ref):
    ends = dot3(matrix, rows)
    low = lanes((3 * K, W)) < 64
    turned = []
    for g in range(NB):
        at = slice(g * W, (g + 1) * W)
        parts = []
        for d in range(3):
            pair = jnp.concatenate([ends[d * K : d * K + K, at], ends[24 + d * K : 24 + d * K + K, at]], axis=0)
            parts.append(pltpu.roll(times(pair, turn_ref[g, d * W : (d + 1) * W, :]), 64, 1))
        front = jnp.concatenate([p[:K] for p in parts], axis=0)
        behind = jnp.concatenate([p[K:] for p in parts], axis=0)
        turned.append((front, behind))
    moved = []
    for g in range(NB):
        both = [jnp.where(low, before, here) for before, here in zip(turned[g - 1], turned[g])]
        moved.append(pltpu.roll(times(jnp.concatenate(both, axis=1), move_ref[g]), 64, 1))
    out = []
    for g in range(NB):
        z = jnp.where(low, moved[g], moved[(g + 1) % NB])
        flat = jnp.concatenate([z[d * K : d * K + K] for d in range(3)], axis=1)
        out.append(times(flat, back_ref[g]))
    return out


def start_all(sources, targets, sem):
    copies = [pltpu.make_async_copy(a, b, sem.at[i]) for i, (a, b) in enumerate(zip(sources, targets))]
    for copy in copies:
        copy.start()
    return copies


def first_kernel(
    own_ref, core_ref, side_ref, square_ref, turn_ref, move_ref, back_ref, mie_ref, member_ref,
    matrix_ref, field_ref, next_ref, sums_ref,
):
    refs = [r.at[i] for r in (own_ref, core_ref, side_ref) for i in range(5)]
    matrix = pair_matrix([(r[:, C : C + W], r[:, C + W : C + 2 * W]) for r in refs])
    matrix_ref[...] = matrix
    rows = jnp.concatenate([r[:, :C] for r in refs], axis=0)
    field = field_of(matrix, rows, turn_ref, move_ref, back_ref)
    spheres = member_ref.shape[1]
    member = (sublanes((K, spheres)) == member_ref[...]).astype(F32)
    count = jnp.sum(member, axis=1, keepdims=True)
    inner = jnp.zeros((K, W), F32)
    square = jnp.zeros((K, W), F32)
    for g in range(NB):
        at = slice(g * W, (g + 1) * W)
        scaled = field[g] * mie_ref[g : g + 1, :]
        total = scaled * count
        field_ref[:, at] = scaled
        next_ref[:, at] = total
        inner = inner + scaled * own_ref[0, :, at]
        square = square + scaled * total
    row = sublanes((K, W))
    inner = jnp.sum(inner, axis=0, keepdims=True)
    square = jnp.sum(square, axis=0, keepdims=True)
    sums_ref[...] = jnp.where(row == 0, square_ref[...], jnp.where(row == 1, inner, jnp.where(row == 2, square, 0.0)))


def second_kernel(
    own_ref, core_ref, side_ref, matrix_ref, turn_ref, move_ref, back_ref, mie_ref, member_ref, first_ref,
    near_ref, next_ref,
):
    core = [core_ref[i * K : i * K + K, :] for i in range(5)]
    rows = jnp.concatenate([own_ref[i] for i in range(5)] + core + [side_ref[i] for i in range(5)], axis=0)
    field = field_of(matrix_ref[...], rows, turn_ref, move_ref, back_ref)
    spheres = member_ref.shape[1]
    member = (sublanes((K, spheres)) == member_ref[...]).astype(F32)
    for g in range(NB):
        at = slice(g * W, (g + 1) * W)
        near_ref[:, at] = rows_of(member, first_ref[:, at])
        next_ref[:, at] = rows_of(member, field[g] * mie_ref[g : g + 1, :])


def last_kernel(entries, rhs_ref, first_ref, second_ref, sums_ref, basis_ref, image_ref):
    sums = jnp.sum(sums_ref[...], axis=1, keepdims=True) / entries
    s, t, u = sums[0:1], sums[1:2], sums[2:3]
    scale2 = s + 1e-06
    rest = (1e-06 + t) / scale2
    norm = jnp.sqrt((rest * rest * s - 2.0 * rest * t + u) / scale2 + 1e-06)
    factor = 1.0 / (norm * jnp.sqrt(scale2))
    first = first_ref[...] * factor
    basis = (rest * factor) * rhs_ref[...] - first
    basis_ref[...] = basis
    image_ref[...] = basis - (rest * first - second_ref[...] * factor)


def call(kernel, out_shape, vmem, anywhere=0, scratch=(), smem=0, work=0):
    space = [pl.BlockSpec(memory_space=pltpu.SMEM)] * smem + [pl.BlockSpec(memory_space=pltpu.VMEM)] * vmem
    space += [pl.BlockSpec(memory_space=pltpu.HBM)] * anywhere
    run = pl.pallas_call(
        kernel,
        out_shape=out_shape,
        in_specs=space,
        scratch_shapes=list(scratch),
        compiler_params=pltpu.CompilerParams(vmem_limit_bytes=VMEM_LIMIT),
        cost_estimate=pl.CostEstimate(flops=work, bytes_accessed=0, transcendentals=0) if work else None,
    )

    def placed(*operands):
        held = [pltpu.with_memory_space_constraint(v, pltpu.HBM) for v in operands[smem + vmem :]]
        return run(*operands[: smem + vmem], *held)

    return placed


def like(*shape):
    return jax.ShapeDtypeStruct(shape, F32)


def swap(v, axis, mask):
    return lax.ppermute(v, axis, [(i, i ^ mask) for i in range(lax.axis_size(axis))])


def row_pairs():
    length = lax.axis_size("z")
    devices = 4 * length
    inside = [(4 * z + 1, 4 * z + 2) for z in range(length)]
    odd = inside + [(4 * z + 3, (4 * z + 4) % devices) for z in range(length)]
    wide = [(4 * z + i, (4 * z + i + 2) % devices) for z in range(length) for i in (2, 3)]
    return [odd + [(b, a) for a, b in odd], wide + [(b, a) for a, b in wide]]


def beside(v):
    odd, wide = row_pairs()
    return swap(v, "x", 1), lax.ppermute(v, ROW, odd), swap(v, "x", 2), lax.ppermute(v, ROW, wide)


def over_side(line):
    devices = lax.axis_size(COL)
    steps = [(i, (i + 1) % devices) for i in range(1, devices, 2)]
    return lax.ppermute(line, COL, steps + [(b, a) for a, b in steps])


def after(v, other):
    return lax.optimization_barrier((v, other))[0]


def plus(v, axis, masks):
    return functools.reduce(jnp.add, [v] + [swap(v, axis, mask) for mask in masks])


def body(rhs, membership, pair_ends, pair_dir, pair_reach, pair_count, send_idx, rotation, translation, mie):
    spheres = rhs.shape[0]
    pairs = pair_dir.shape[0]
    member = membership.reshape(1, spheres)
    mie = mie.reshape(NB, W)
    whole = [
        pltpu.VMEM((1, spheres), jnp.int32),
        pltpu.VMEM((2, pairs), jnp.int32),
        pltpu.VMEM((1, pairs), jnp.int32),
        pltpu.VMEM((1, pairs), F32),
        pltpu.VMEM((CAP, NPEER), jnp.int32),
        pltpu.SemaphoreType.DMA((6,)),
    ]
    packed, squares, kept = call(
        gather_kernel,
        (like(K, C + EXTRA), like(1, W), like(spheres, C)),
        0,
        6,
        [pltpu.VMEM((K, W), F32)] + whole,
        1,
    )(
        pair_count,
        rhs,
        member,
        pair_ends.T,
        pair_dir.reshape(1, pairs),
        pair_reach.reshape(1, pairs),
        jnp.transpose(send_idx, (0, 2, 1)).reshape(CAP, NPEER),
    )
    weights = call(
        split_kernel,
        tuple(jax.ShapeDtypeStruct((NB, rows * W, 2 * W), BF16) for rows in (3, 2, 3)),
        0,
        2,
        [pltpu.VMEM(rotation.shape, F32), pltpu.VMEM(translation.shape, F32), pltpu.SemaphoreType.DMA((2,))],
        work=3 * 10**9,
    )(rotation, translation)
    line = jnp.stack((packed,) + beside(packed))
    matrix, first, following, sums = call(
        first_kernel, (like(6 * K, 15 * K), like(K, C), like(K, C), like(K, W)), 9
    )(
        line, swap(line, "c", 1), over_side(line), squares, *weights, mie, member
    )
    odd, wide = row_pairs()
    far = lax.ppermute(following, ROW, wide)
    following = jnp.concatenate([following, plus(sums, "z", (1,))], axis=1)
    near = (swap(following, "x", 1), lax.ppermute(following, ROW, odd), swap(following, "x", 2), far)
    line = jnp.stack([v[:, :C] for v in (following,) + near])
    sums = after(sum(v[:, C:] for v in near[:3]) + following[:, C:], near[3])
    carried = jnp.concatenate([line.reshape(5 * K, C), jnp.pad(sums, ((0, 0), (0, C - W)))], axis=0)
    core = swap(carried, "c", 1)
    side = over_side(line)
    sums = sums + core[5 * K :, :W]
    near, second = call(second_kernel, (like(spheres, C), like(spheres, C)), 10, work=5 * 10**9)(
        line, core, side, matrix, *weights, mie, member, first
    )
    sums = plus(sums, "z", (2, 6, 4))
    sums = plus(sums, "y", (2, 1, 3))
    entries = float(lax.axis_size(ALL) * spheres * C)
    return tuple(
        call(functools.partial(last_kernel, entries), (like(spheres, C), like(spheres, C)), 4)(
            kept, near, second, sums
        )
    )


def solution(mesh):
    torus = Mesh(mesh.devices.reshape(4, 2, 8, 4), ALL)
    return jax.shard_map(
        body,
        mesh=torus,
        in_specs=(
            P(ALL, None),
            P(ALL),
            P(ALL, None),
            P(ALL),
            P(ALL),
            P(ALL),
            P(ALL, None, None),
            P(),
            P(),
            P(),
        ),
        out_specs=(P(ALL, None), P(ALL, None)),
        check_vma=False,
    )
```

```python
import functools

import jax
import jax.numpy as jnp
from jax import lax
from jax.experimental import pallas as pl
from jax.experimental.pallas import tpu as pltpu
from jax.sharding import Mesh
from jax.sharding import PartitionSpec as P

F32 = jnp.float32
BF16 = jnp.bfloat16
ALL = ("y", "c", "z", "x")
ROW = ("z", "x")
COL = ("y", "c")
K = 8
C = 1920
NB = 15
W = 128
NPEER = 14
CAP = 4
EXTRA = 256
VMEM_LIMIT = 24 * 1024 * 1024

NN = (((1,), (0,)), ((), ()))
NT = (((1,), (1,)), ((), ()))
TN = (((0,), (0,)), ((), ()))


def halves(x):
    high = x.astype(BF16)
    return high, (x - high.astype(F32)).astype(BF16)


def dot3(a, b, dims=NN):
    rows = a.shape[0]
    a_high32 = a.astype(BF16).astype(F32)
    both = jnp.concatenate([a_high32, a - a_high32], axis=0).astype(BF16)
    b_high, b_low = halves(b)
    first = lax.dot_general(both, b_high, dims, preferred_element_type=F32)
    second = lax.dot_general(a.astype(BF16), b_low, dims, preferred_element_type=F32)
    return first[:rows] + first[rows:] + second


def thirds(x):
    high = x.astype(BF16).astype(F32)
    rest = x - high
    middle = rest.astype(BF16).astype(F32)
    return high, middle, rest - middle


def weighted_hot(x, hot):
    rows = x.shape[0]
    out = lax.dot_general(
        jnp.concatenate(thirds(x), axis=0).astype(BF16), hot.astype(BF16), NT, preferred_element_type=F32
    )
    return out[:rows] + out[rows : 2 * rows] + out[2 * rows :]


def hot_times(hot, x, dims=NN):
    hot = hot.astype(BF16)
    return sum(lax.dot_general(hot, part.astype(BF16), dims, preferred_element_type=F32) for part in thirds(x))


def rows_of(member, x):
    return lax.dot_general(
        jnp.concatenate([member] * 3, axis=0).astype(BF16),
        jnp.concatenate(thirds(x), axis=0).astype(BF16),
        TN,
        preferred_element_type=F32,
    )


def lanes(shape):
    return lax.broadcasted_iota(jnp.int32, shape, 1)


def sublanes(shape):
    return lax.broadcasted_iota(jnp.int32, shape, 0)


def gather_kernel(count_ref, *refs):
    sources, (out_ref, square_ref, rhs_ref), (pad_ref, member_ref, ends_ref, dir_ref, reach_ref, send_ref, sem) = (
        refs[:6],
        refs[6:9],
        refs[9:],
    )
    targets = (rhs_ref, member_ref, ends_ref, dir_ref, reach_ref, send_ref)
    copies = [pltpu.make_async_copy(a, b, sem.at[i]) for i, (a, b) in enumerate(zip(sources, targets))]
    for copy in copies:
        copy.start()
    for copy in copies:
        copy.wait()
    spheres = rhs_ref.shape[0]
    pairs = dir_ref.shape[1]
    rhs = rhs_ref[...]
    member = (sublanes((K, spheres)) == member_ref[...]).astype(F32)
    out_ref[:, :C] = hot_times(member, rhs)
    squares = jnp.sum(rhs * rhs, axis=0, keepdims=True)
    partial = squares[:, :W]
    for g in range(1, NB):
        partial = partial + squares[:, g * W : (g + 1) * W]
    square_ref[...] = partial
    weight = jnp.where(lanes((1, pairs)) < count_ref[0], reach_ref[...], 0.0)
    own = ends_ref[0:1, :]
    near = ends_ref[1:2, :]
    far = near - K
    place = jnp.where(near < K, near, K + NPEER * (far & (CAP - 1)) + (far >> 2))
    rows = sublanes((W, pairs)) & 63
    near_hot = (rows == place).astype(F32)
    own_weight = jnp.where(sublanes((K, pairs)) == own, weight, 0.0)
    lane = lanes((K, W))
    classes = jnp.concatenate([jnp.where(dir_ref[...] == d, own_weight, 0.0) for d in range(3)], axis=0)
    table = weighted_hot(classes, near_hot)
    blocks = [table[d * K : d * K + K] for d in range(3)]
    pad_ref[...] = jnp.zeros_like(pad_ref)
    pad_ref[0:CAP, 0:NPEER] = send_ref[...].astype(F32)
    names = jnp.where(lane < 64 + K, (lane - 64).astype(F32), 0.0)
    for slot in range(CAP):
        row = jnp.broadcast_to(pad_ref[slot : slot + 1, :], (K, W))
        names = names + pltpu.roll(row, 64 + K + NPEER * slot, 1)
    out_ref[:, C : C + W] = jnp.where(lane < 64, blocks[0], blocks[1])
    out_ref[:, C + W :] = jnp.where(lane < 64, blocks[2], names)


def pair_matrix(units):
    x = lax.axis_index("x")
    c = lax.axis_index("c")
    core = 1 - 2 * c
    one = 1 - 2 * (x & 1)
    two = jnp.where(x < 2, 2, -2)
    lane = lanes((K, W))
    low = lane < 64
    half = lane & 63
    seen = half - K
    peer = seen - NPEER * (
        (seen >= NPEER).astype(jnp.int32)
        + (seen >= 2 * NPEER).astype(jnp.int32)
        + (seen >= 3 * NPEER).astype(jnp.int32)
    )
    peer = jnp.where(half < K, -1, peer)
    names_of = sublanes((K, W)).astype(F32)
    hot, first, second = [], [], []
    for group, d_row in enumerate((0, core, -core)):
        for place, d_col in enumerate((0, one, -one, two, -two)):
            v0, v1 = units[group * 5 + place]
            names = jnp.where(low, pltpu.roll(v1, 64, 1), v1)
            if group == 0 and place == 0:
                here = peer == -1
                there = here
                own_hot = jnp.where(names == names_of, 1.0, 0.0)
            else:
                f = (1 - d_row) * 5 + 2 - d_col
                b = 14 - f
                here = peer == f - (f > 7).astype(jnp.int32)
                there = peer == b - (b > 7).astype(jnp.int32)
            hot.append(jnp.where((names == names_of) & here, 1.0, 0.0))
            first.append(jnp.where(there, v0, 0.0))
            second.append(jnp.where(there & low, v1, 0.0))
    hot = jnp.concatenate(hot, axis=0)
    first = jnp.concatenate(first, axis=0)
    second = jnp.concatenate(second, axis=0)
    v0, v1 = units[0]

    def two_classes(v):
        return jnp.concatenate([jnp.where(low, v, 0.0), jnp.where(low, 0.0, v)], axis=0)

    ends = jnp.concatenate([two_classes(v0), jnp.where(low, v1, 0.0)], axis=0)
    return jnp.concatenate(
        [
            weighted_hot(ends, hot),
            hot_times(two_classes(own_hot), first, NT),
            hot_times(jnp.where(low, own_hot, 0.0), second, NT),
        ],
        axis=0,
    )


def stacked(x):
    high = x.astype(BF16).astype(F32)
    return jnp.concatenate([high, x - high], axis=0).astype(BF16)


def times(x, parts):
    rows, columns = x.shape[0], parts.shape[1] // 2
    out = lax.dot_general(stacked(x), parts, NN, preferred_element_type=F32)
    return out[:rows, :columns] + (out[:rows, columns:] + out[rows:, :columns]) + out[rows:, columns:]


def split_kernel(rotation_any, translation_any, turn_ref, move_ref, back_ref, rotation_ref, translation_ref, sem):
    copies = start_all((rotation_any, translation_any), (rotation_ref, translation_ref), sem)

    def put(ref, g, row, w):
        ref[g, row : row + W, :] = jnp.concatenate(halves(w), axis=1)

    copies[0].wait()
    for g in range(NB):
        for d in range(3):
            w = rotation_ref[d, g]
            put(turn_ref, g, d * W, w)
            put(back_ref, g, d * W, w.T)
    copies[1].wait()
    for g in range(NB):
        w = translation_ref[g]
        put(move_ref, g, 0, w)
        put(move_ref, g, W, w.T)


def field_of(matrix, rows, turn_ref, move_ref, back_ref):
    ends = dot3(matrix, rows)
    low = lanes((3 * K, W)) < 64
    turned = []
    for g in range(NB):
        at = slice(g * W, (g + 1) * W)
        parts = []
        for d in range(3):
            pair = jnp.concatenate([ends[d * K : d * K + K, at], ends[24 + d * K : 24 + d * K + K, at]], axis=0)
            parts.append(pltpu.roll(times(pair, turn_ref[g, d * W : (d + 1) * W, :]), 64, 1))
        front = jnp.concatenate([p[:K] for p in parts], axis=0)
        behind = jnp.concatenate([p[K:] for p in parts], axis=0)
        turned.append((front, behind))
    moved = []
    for g in range(NB):
        both = [jnp.where(low, before, here) for before, here in zip(turned[g - 1], turned[g])]
        moved.append(pltpu.roll(times(jnp.concatenate(both, axis=1), move_ref[g]), 64, 1))
    out = []
    for g in range(NB):
        z = jnp.where(low, moved[g], moved[(g + 1) % NB])
        flat = jnp.concatenate([z[d * K : d * K + K] for d in range(3)], axis=1)
        out.append(times(flat, back_ref[g]))
    return out


def start_all(sources, targets, sem):
    copies = [pltpu.make_async_copy(a, b, sem.at[i]) for i, (a, b) in enumerate(zip(sources, targets))]
    for copy in copies:
        copy.start()
    return copies


def first_kernel(
    own_ref, core_ref, wide_ref, close_ref, square_ref, turn_ref, move_ref, back_ref, mie_ref, member_ref,
    matrix_ref, field_ref, next_ref, sums_ref,
):
    refs = [r.at[i] for r in (own_ref, core_ref) for i in range(5)]
    refs += [wide_ref.at[0], close_ref.at[0], close_ref.at[1], wide_ref.at[1], wide_ref.at[2]]
    matrix = pair_matrix([(r[:, C : C + W], r[:, C + W : C + 2 * W]) for r in refs])
    matrix_ref[...] = matrix
    rows = jnp.concatenate([r[:, :C] for r in refs], axis=0)
    field = field_of(matrix, rows, turn_ref, move_ref, back_ref)
    spheres = member_ref.shape[1]
    member = (sublanes((K, spheres)) == member_ref[...]).astype(F32)
    count = jnp.sum(member, axis=1, keepdims=True)
    inner = jnp.zeros((K, W), F32)
    square = jnp.zeros((K, W), F32)
    for g in range(NB):
        at = slice(g * W, (g + 1) * W)
        scaled = field[g] * mie_ref[g : g + 1, :]
        total = scaled * count
        field_ref[:, at] = scaled
        next_ref[:, at] = total
        inner = inner + scaled * own_ref[0, :, at]
        square = square + scaled * total
    row = sublanes((K, W))
    inner = jnp.sum(inner, axis=0, keepdims=True)
    square = jnp.sum(square, axis=0, keepdims=True)
    sums_ref[...] = jnp.where(row == 0, square_ref[...], jnp.where(row == 1, inner, jnp.where(row == 2, square, 0.0)))


def second_kernel(
    own_ref, core_ref, side_ref, matrix_ref, turn_ref, move_ref, back_ref, mie_ref, member_ref, first_ref,
    near_ref, next_ref,
):
    core = [core_ref[i * K : i * K + K, :] for i in range(5)]
    rows = jnp.concatenate([own_ref[i] for i in range(5)] + core + [side_ref[i] for i in range(5)], axis=0)
    field = field_of(matrix_ref[...], rows, turn_ref, move_ref, back_ref)
    spheres = member_ref.shape[1]
    member = (sublanes((K, spheres)) == member_ref[...]).astype(F32)
    for g in range(NB):
        at = slice(g * W, (g + 1) * W)
        near_ref[:, at] = rows_of(member, first_ref[:, at])
        next_ref[:, at] = rows_of(member, field[g] * mie_ref[g : g + 1, :])


def last_kernel(entries, rhs_ref, first_ref, second_ref, sums_ref, basis_ref, image_ref):
    sums = jnp.sum(sums_ref[...], axis=1, keepdims=True) / entries
    s, t, u = sums[0:1], sums[1:2], sums[2:3]
    scale2 = s + 1e-06
    rest = (1e-06 + t) / scale2
    norm = jnp.sqrt((rest * rest * s - 2.0 * rest * t + u) / scale2 + 1e-06)
    factor = 1.0 / (norm * jnp.sqrt(scale2))
    first = first_ref[...] * factor
    basis = (rest * factor) * rhs_ref[...] - first
    basis_ref[...] = basis
    image_ref[...] = basis - (rest * first - second_ref[...] * factor)


def call(kernel, out_shape, vmem, anywhere=0, scratch=(), smem=0, work=0):
    space = [pl.BlockSpec(memory_space=pltpu.SMEM)] * smem + [pl.BlockSpec(memory_space=pltpu.VMEM)] * vmem
    space += [pl.BlockSpec(memory_space=pltpu.HBM)] * anywhere
    run = pl.pallas_call(
        kernel,
        out_shape=out_shape,
        in_specs=space,
        scratch_shapes=list(scratch),
        compiler_params=pltpu.CompilerParams(vmem_limit_bytes=VMEM_LIMIT),
        cost_estimate=pl.CostEstimate(flops=work, bytes_accessed=0, transcendentals=0) if work else None,
    )

    def placed(*operands):
        held = [pltpu.with_memory_space_constraint(v, pltpu.HBM) for v in operands[smem + vmem :]]
        return run(*operands[: smem + vmem], *held)

    return placed


def like(*shape):
    return jax.ShapeDtypeStruct(shape, F32)


def swap(v, axis, mask):
    return lax.ppermute(v, axis, [(i, i ^ mask) for i in range(lax.axis_size(axis))])


def row_pairs():
    length = lax.axis_size("z")
    devices = 4 * length
    inside = [(4 * z + 1, 4 * z + 2) for z in range(length)]
    odd = inside + [(4 * z + 3, (4 * z + 4) % devices) for z in range(length)]
    wide = [(4 * z + i, (4 * z + i + 2) % devices) for z in range(length) for i in (2, 3)]
    return [odd + [(b, a) for a, b in odd], wide + [(b, a) for a, b in wide]]


def beside(v):
    odd, wide = row_pairs()
    return swap(v, "x", 1), lax.ppermute(v, ROW, odd), swap(v, "x", 2), lax.ppermute(v, ROW, wide)


def over_side(line):
    devices = lax.axis_size(COL)
    steps = [(i, (i + 1) % devices) for i in range(1, devices, 2)]
    return lax.ppermute(line, COL, steps + [(b, a) for a, b in steps])


def after(v, other):
    return lax.optimization_barrier((v, other))[0]


def plus(v, axis, masks):
    return functools.reduce(jnp.add, [v] + [swap(v, axis, mask) for mask in masks])


def body(rhs, membership, pair_ends, pair_dir, pair_reach, pair_count, send_idx, rotation, translation, mie):
    spheres = rhs.shape[0]
    pairs = pair_dir.shape[0]
    member = membership.reshape(1, spheres)
    mie = mie.reshape(NB, W)
    whole = [
        pltpu.VMEM((1, spheres), jnp.int32),
        pltpu.VMEM((2, pairs), jnp.int32),
        pltpu.VMEM((1, pairs), jnp.int32),
        pltpu.VMEM((1, pairs), F32),
        pltpu.VMEM((CAP, NPEER), jnp.int32),
        pltpu.SemaphoreType.DMA((6,)),
    ]
    packed, squares, kept = call(
        gather_kernel,
        (like(K, C + EXTRA), like(1, W), like(spheres, C)),
        0,
        6,
        [pltpu.VMEM((K, W), F32)] + whole,
        1,
    )(
        pair_count,
        rhs,
        member,
        pair_ends.T,
        pair_dir.reshape(1, pairs),
        pair_reach.reshape(1, pairs),
        jnp.transpose(send_idx, (0, 2, 1)).reshape(CAP, NPEER),
    )
    weights = call(
        split_kernel,
        tuple(jax.ShapeDtypeStruct((NB, rows * W, 2 * W), BF16) for rows in (3, 2, 3)),
        0,
        2,
        [pltpu.VMEM(rotation.shape, F32), pltpu.VMEM(translation.shape, F32), pltpu.SemaphoreType.DMA((2,))],
        work=3 * 10**9,
    )(rotation, translation)
    one, back_one, two, back_two = beside(packed)
    wide_side = over_side(jnp.stack([packed, two, back_two]))
    close_side = over_side(after(jnp.stack([one, back_one]), weights[1]))
    line = jnp.stack([packed, one, back_one, two, back_two])
    matrix, first, following, sums = call(
        first_kernel, (like(6 * K, 15 * K), like(K, C), like(K, C), like(K, W)), 10
    )(
        line, swap(line, "c", 1), wide_side, close_side, squares, *weights, mie, member
    )
    odd, wide = row_pairs()
    far = lax.ppermute(following, ROW, wide)
    following = jnp.concatenate([following, plus(sums, "z", (1,))], axis=1)
    near = (swap(following, "x", 1), lax.ppermute(following, ROW, odd), swap(following, "x", 2), far)
    line = jnp.stack([v[:, :C] for v in (following,) + near])
    sums = after(sum(v[:, C:] for v in near[:3]) + following[:, C:], near[3])
    carried = jnp.concatenate([line.reshape(5 * K, C), jnp.pad(sums, ((0, 0), (0, C - W)))], axis=0)
    core = swap(carried, "c", 1)
    side = over_side(line)
    sums = sums + core[5 * K :, :W]
    near, second = call(second_kernel, (like(spheres, C), like(spheres, C)), 10, work=5 * 10**9)(
        line, core, side, matrix, *weights, mie, member, first
    )
    sums = plus(sums, "z", (2, 6, 4))
    sums = plus(sums, "y", (2, 1, 3))
    entries = float(lax.axis_size(ALL) * spheres * C)
    return tuple(
        call(functools.partial(last_kernel, entries), (like(spheres, C), like(spheres, C)), 4)(
            kept, near, second, sums
        )
    )


def solution(mesh):
    torus = Mesh(mesh.devices.reshape(4, 2, 8, 4), ALL)
    return jax.shard_map(
        body,
        mesh=torus,
        in_specs=(
            P(ALL, None),
            P(ALL),
            P(ALL, None),
            P(ALL),
            P(ALL),
            P(ALL),
            P(ALL, None, None),
            P(),
            P(),
            P(),
        ),
        out_specs=(P(ALL, None), P(ALL, None)),
        check_vma=False,
    )
```

```python
import functools

import jax
import jax.numpy as jnp
from jax import lax
from jax.experimental import pallas as pl
from jax.experimental.pallas import tpu as pltpu
from jax.sharding import Mesh
from jax.sharding import PartitionSpec as P

F32 = jnp.float32
BF16 = jnp.bfloat16
ALL = ("y", "c", "z", "x")
ROW = ("z", "x")
COL = ("y", "c")
K = 8
C = 1920
NB = 15
W = 128
NPEER = 14
CAP = 4
EXTRA = 256
VMEM_LIMIT = 24 * 1024 * 1024

NN = (((1,), (0,)), ((), ()))
NT = (((1,), (1,)), ((), ()))
TN = (((0,), (0,)), ((), ()))


def halves(x):
    high = x.astype(BF16)
    return high, (x - high.astype(F32)).astype(BF16)


def dot3(a, b, dims=NN):
    rows = a.shape[0]
    a_high32 = a.astype(BF16).astype(F32)
    both = jnp.concatenate([a_high32, a - a_high32], axis=0).astype(BF16)
    b_high, b_low = halves(b)
    first = lax.dot_general(both, b_high, dims, preferred_element_type=F32)
    second = lax.dot_general(a.astype(BF16), b_low, dims, preferred_element_type=F32)
    return first[:rows] + first[rows:] + second


def thirds(x):
    high = x.astype(BF16).astype(F32)
    rest = x - high
    middle = rest.astype(BF16).astype(F32)
    return high, middle, rest - middle


def weighted_hot(x, hot):
    rows = x.shape[0]
    out = lax.dot_general(
        jnp.concatenate(thirds(x), axis=0).astype(BF16), hot.astype(BF16), NT, preferred_element_type=F32
    )
    return out[:rows] + out[rows : 2 * rows] + out[2 * rows :]


def hot_times(hot, x, dims=NN):
    hot = hot.astype(BF16)
    return sum(lax.dot_general(hot, part.astype(BF16), dims, preferred_element_type=F32) for part in thirds(x))


def rows_of(member, x):
    return lax.dot_general(
        jnp.concatenate([member] * 3, axis=0).astype(BF16),
        jnp.concatenate(thirds(x), axis=0).astype(BF16),
        TN,
        preferred_element_type=F32,
    )


def lanes(shape):
    return lax.broadcasted_iota(jnp.int32, shape, 1)


def sublanes(shape):
    return lax.broadcasted_iota(jnp.int32, shape, 0)


def gather_kernel(count_ref, *refs):
    sources, (out_ref, square_ref, rhs_ref), (pad_ref, member_ref, ends_ref, dir_ref, reach_ref, send_ref, sem) = (
        refs[:6],
        refs[6:9],
        refs[9:],
    )
    targets = (rhs_ref, member_ref, ends_ref, dir_ref, reach_ref, send_ref)
    copies = [pltpu.make_async_copy(a, b, sem.at[i]) for i, (a, b) in enumerate(zip(sources, targets))]
    for copy in copies:
        copy.start()
    for copy in copies[1:]:
        copy.wait()
    spheres = rhs_ref.shape[0]
    pairs = dir_ref.shape[1]
    weight = jnp.where(lanes((1, pairs)) < count_ref[0], reach_ref[...], 0.0)
    own = ends_ref[0:1, :]
    near = ends_ref[1:2, :]
    far = near - K
    place = jnp.where(near < K, near, K + NPEER * (far & (CAP - 1)) + (far >> 2))
    rows = sublanes((W, pairs)) & 63
    near_hot = (rows == place).astype(F32)
    own_weight = jnp.where(sublanes((K, pairs)) == own, weight, 0.0)
    lane = lanes((K, W))
    classes = jnp.concatenate([jnp.where(dir_ref[...] == d, own_weight, 0.0) for d in range(3)], axis=0)
    table = weighted_hot(classes, near_hot)
    blocks = [table[d * K : d * K + K] for d in range(3)]
    pad_ref[...] = jnp.zeros_like(pad_ref)
    pad_ref[0:CAP, 0:NPEER] = send_ref[...].astype(F32)
    names = jnp.where(lane < 64 + K, (lane - 64).astype(F32), 0.0)
    for slot in range(CAP):
        row = jnp.broadcast_to(pad_ref[slot : slot + 1, :], (K, W))
        names = names + pltpu.roll(row, 64 + K + NPEER * slot, 1)
    out_ref[:, C : C + W] = jnp.where(lane < 64, blocks[0], blocks[1])
    out_ref[:, C + W :] = jnp.where(lane < 64, blocks[2], names)
    copies[0].wait()
    rhs = rhs_ref[...]
    member = (sublanes((K, spheres)) == member_ref[...]).astype(F32)
    out_ref[:, :C] = hot_times(member, rhs)
    squares = jnp.sum(rhs * rhs, axis=0, keepdims=True)
    partial = squares[:, :W]
    for g in range(1, NB):
        partial = partial + squares[:, g * W : (g + 1) * W]
    square_ref[...] = partial


def pair_matrix(units):
    x = lax.axis_index("x")
    c = lax.axis_index("c")
    core = 1 - 2 * c
    one = 1 - 2 * (x & 1)
    two = jnp.where(x < 2, 2, -2)
    lane = lanes((K, W))
    low = lane < 64
    half = lane & 63
    seen = half - K
    peer = seen - NPEER * (
        (seen >= NPEER).astype(jnp.int32)
        + (seen >= 2 * NPEER).astype(jnp.int32)
        + (seen >= 3 * NPEER).astype(jnp.int32)
    )
    peer = jnp.where(half < K, -1, peer)
    names_of = sublanes((K, W)).astype(F32)
    hot, first, second = [], [], []
    for group, d_row in enumerate((0, core, -core)):
        for place, d_col in enumerate((0, one, -one, two, -two)):
            v0, v1 = units[group * 5 + place]
            names = jnp.where(low, pltpu.roll(v1, 64, 1), v1)
            if group == 0 and place == 0:
                here = peer == -1
                there = here
                own_hot = jnp.where(names == names_of, 1.0, 0.0)
            else:
                f = (1 - d_row) * 5 + 2 - d_col
                b = 14 - f
                here = peer == f - (f > 7).astype(jnp.int32)
                there = peer == b - (b > 7).astype(jnp.int32)
            hot.append(jnp.where((names == names_of) & here, 1.0, 0.0))
            first.append(jnp.where(there, v0, 0.0))
            second.append(jnp.where(there & low, v1, 0.0))
    hot = jnp.concatenate(hot, axis=0)
    first = jnp.concatenate(first, axis=0)
    second = jnp.concatenate(second, axis=0)
    v0, v1 = units[0]

    def two_classes(v):
        return jnp.concatenate([jnp.where(low, v, 0.0), jnp.where(low, 0.0, v)], axis=0)

    ends = jnp.concatenate([two_classes(v0), jnp.where(low, v1, 0.0)], axis=0)
    return jnp.concatenate(
        [
            weighted_hot(ends, hot),
            hot_times(two_classes(own_hot), first, NT),
            hot_times(jnp.where(low, own_hot, 0.0), second, NT),
        ],
        axis=0,
    )


def stacked(x):
    high = x.astype(BF16).astype(F32)
    return jnp.concatenate([high, x - high], axis=0).astype(BF16)


def times(x, parts):
    rows, columns = x.shape[0], parts.shape[1] // 2
    out = lax.dot_general(stacked(x), parts, NN, preferred_element_type=F32)
    return out[:rows, :columns] + (out[:rows, columns:] + out[rows:, :columns]) + out[rows:, columns:]


def split_kernel(rotation_any, translation_any, turn_ref, move_ref, back_ref, rotation_ref, translation_ref, sem):
    copies = start_all((rotation_any, translation_any), (rotation_ref, translation_ref), sem)

    def put(ref, g, row, w):
        ref[g, row : row + W, :] = jnp.concatenate(halves(w), axis=1)

    copies[0].wait()
    for g in range(NB):
        for d in range(3):
            w = rotation_ref[d, g]
            put(turn_ref, g, d * W, w)
            put(back_ref, g, d * W, w.T)
    copies[1].wait()
    for g in range(NB):
        w = translation_ref[g]
        put(move_ref, g, 0, w)
        put(move_ref, g, W, w.T)


def field_of(matrix, rows, turn_ref, move_ref, back_ref):
    ends = dot3(matrix, rows)
    low = lanes((3 * K, W)) < 64
    turned = []
    for g in range(NB):
        at = slice(g * W, (g + 1) * W)
        parts = []
        for d in range(3):
            pair = jnp.concatenate([ends[d * K : d * K + K, at], ends[24 + d * K : 24 + d * K + K, at]], axis=0)
            parts.append(pltpu.roll(times(pair, turn_ref[g, d * W : (d + 1) * W, :]), 64, 1))
        front = jnp.concatenate([p[:K] for p in parts], axis=0)
        behind = jnp.concatenate([p[K:] for p in parts], axis=0)
        turned.append((front, behind))
    moved = []
    for g in range(NB):
        both = [jnp.where(low, before, here) for before, here in zip(turned[g - 1], turned[g])]
        moved.append(pltpu.roll(times(jnp.concatenate(both, axis=1), move_ref[g]), 64, 1))
    out = []
    for g in range(NB):
        z = jnp.where(low, moved[g], moved[(g + 1) % NB])
        flat = jnp.concatenate([z[d * K : d * K + K] for d in range(3)], axis=1)
        out.append(times(flat, back_ref[g]))
    return out


def start_all(sources, targets, sem):
    copies = [pltpu.make_async_copy(a, b, sem.at[i]) for i, (a, b) in enumerate(zip(sources, targets))]
    for copy in copies:
        copy.start()
    return copies


def first_kernel(
    own_ref, core_ref, side_ref, square_ref, turn_ref, move_ref, back_ref, mie_ref, member_ref,
    matrix_ref, field_ref, next_ref, sums_ref,
):
    refs = [r.at[i] for r in (own_ref, core_ref, side_ref) for i in range(5)]
    matrix = pair_matrix([(r[:, C : C + W], r[:, C + W : C + 2 * W]) for r in refs])
    matrix_ref[...] = matrix
    rows = jnp.concatenate([r[:, :C] for r in refs], axis=0)
    field = field_of(matrix, rows, turn_ref, move_ref, back_ref)
    spheres = member_ref.shape[1]
    member = (sublanes((K, spheres)) == member_ref[...]).astype(F32)
    count = jnp.sum(member, axis=1, keepdims=True)
    inner = jnp.zeros((K, W), F32)
    square = jnp.zeros((K, W), F32)
    for g in range(NB):
        at = slice(g * W, (g + 1) * W)
        scaled = field[g] * mie_ref[g : g + 1, :]
        total = scaled * count
        field_ref[:, at] = scaled
        next_ref[:, at] = total
        inner = inner + scaled * own_ref[0, :, at]
        square = square + scaled * total
    row = sublanes((K, W))
    inner = jnp.sum(inner, axis=0, keepdims=True)
    square = jnp.sum(square, axis=0, keepdims=True)
    sums_ref[...] = jnp.where(row == 0, square_ref[...], jnp.where(row == 1, inner, jnp.where(row == 2, square, 0.0)))


def second_kernel(
    own_ref, core_ref, side_ref, matrix_ref, turn_ref, move_ref, back_ref, mie_ref, member_ref, first_ref,
    near_ref, next_ref,
):
    core = [core_ref[i * K : i * K + K, :] for i in range(5)]
    rows = jnp.concatenate([own_ref[i] for i in range(5)] + core + [side_ref[i] for i in range(5)], axis=0)
    field = field_of(matrix_ref[...], rows, turn_ref, move_ref, back_ref)
    spheres = member_ref.shape[1]
    member = (sublanes((K, spheres)) == member_ref[...]).astype(F32)
    for g in range(NB):
        at = slice(g * W, (g + 1) * W)
        near_ref[:, at] = rows_of(member, first_ref[:, at])
        next_ref[:, at] = rows_of(member, field[g] * mie_ref[g : g + 1, :])


def last_kernel(entries, rhs_ref, first_ref, second_ref, sums_ref, basis_ref, image_ref):
    sums = jnp.sum(sums_ref[...], axis=1, keepdims=True) / entries
    s, t, u = sums[0:1], sums[1:2], sums[2:3]
    scale2 = s + 1e-06
    rest = (1e-06 + t) / scale2
    norm = jnp.sqrt((rest * rest * s - 2.0 * rest * t + u) / scale2 + 1e-06)
    factor = 1.0 / (norm * jnp.sqrt(scale2))
    first = first_ref[...] * factor
    basis = (rest * factor) * rhs_ref[...] - first
    basis_ref[...] = basis
    image_ref[...] = basis - (rest * first - second_ref[...] * factor)


def call(kernel, out_shape, vmem, anywhere=0, scratch=(), smem=0, work=0):
    space = [pl.BlockSpec(memory_space=pltpu.SMEM)] * smem + [pl.BlockSpec(memory_space=pltpu.VMEM)] * vmem
    space += [pl.BlockSpec(memory_space=pltpu.HBM)] * anywhere
    run = pl.pallas_call(
        kernel,
        out_shape=out_shape,
        in_specs=space,
        scratch_shapes=list(scratch),
        compiler_params=pltpu.CompilerParams(vmem_limit_bytes=VMEM_LIMIT),
        cost_estimate=pl.CostEstimate(flops=work, bytes_accessed=0, transcendentals=0) if work else None,
    )

    def placed(*operands):
        held = [pltpu.with_memory_space_constraint(v, pltpu.HBM) for v in operands[smem + vmem :]]
        return run(*operands[: smem + vmem], *held)

    return placed


def like(*shape):
    return jax.ShapeDtypeStruct(shape, F32)


def swap(v, axis, mask):
    return lax.ppermute(v, axis, [(i, i ^ mask) for i in range(lax.axis_size(axis))])


def row_pairs():
    length = lax.axis_size("z")
    devices = 4 * length
    inside = [(4 * z + 1, 4 * z + 2) for z in range(length)]
    odd = inside + [(4 * z + 3, (4 * z + 4) % devices) for z in range(length)]
    wide = [(4 * z + i, (4 * z + i + 2) % devices) for z in range(length) for i in (2, 3)]
    return [odd + [(b, a) for a, b in odd], wide + [(b, a) for a, b in wide]]


def beside(v):
    odd, wide = row_pairs()
    return swap(v, "x", 1), lax.ppermute(v, ROW, odd), swap(v, "x", 2), lax.ppermute(v, ROW, wide)


def over_side(line):
    devices = lax.axis_size(COL)
    steps = [(i, (i + 1) % devices) for i in range(1, devices, 2)]
    return lax.ppermute(line, COL, steps + [(b, a) for a, b in steps])


def after(v, other):
    return lax.optimization_barrier((v, other))[0]


def plus(v, axis, masks):
    return functools.reduce(jnp.add, [v] + [swap(v, axis, mask) for mask in masks])


def body(rhs, membership, pair_ends, pair_dir, pair_reach, pair_count, send_idx, rotation, translation, mie):
    spheres = rhs.shape[0]
    pairs = pair_dir.shape[0]
    member = membership.reshape(1, spheres)
    mie = mie.reshape(NB, W)
    whole = [
        pltpu.VMEM((1, spheres), jnp.int32),
        pltpu.VMEM((2, pairs), jnp.int32),
        pltpu.VMEM((1, pairs), jnp.int32),
        pltpu.VMEM((1, pairs), F32),
        pltpu.VMEM((CAP, NPEER), jnp.int32),
        pltpu.SemaphoreType.DMA((6,)),
    ]
    packed, squares, kept = call(
        gather_kernel,
        (like(K, C + EXTRA), like(1, W), like(spheres, C)),
        0,
        6,
        [pltpu.VMEM((K, W), F32)] + whole,
        1,
    )(
        pair_count,
        rhs,
        member,
        pair_ends.T,
        pair_dir.reshape(1, pairs),
        pair_reach.reshape(1, pairs),
        jnp.transpose(send_idx, (0, 2, 1)).reshape(CAP, NPEER),
    )
    weights = call(
        split_kernel,
        tuple(jax.ShapeDtypeStruct((NB, rows * W, 2 * W), BF16) for rows in (3, 2, 3)),
        0,
        2,
        [pltpu.VMEM(rotation.shape, F32), pltpu.VMEM(translation.shape, F32), pltpu.SemaphoreType.DMA((2,))],
        work=3 * 10**9,
    )(rotation, translation)
    line = jnp.stack((packed,) + beside(packed))
    matrix, first, following, sums = call(
        first_kernel, (like(6 * K, 15 * K), like(K, C), like(K, C), like(K, W)), 9
    )(
        line, swap(line, "c", 1), over_side(line), squares, *weights, mie, member
    )
    odd, wide = row_pairs()
    far = lax.ppermute(following, ROW, wide)
    following = jnp.concatenate([following, plus(sums, "z", (1,))], axis=1)
    near = (swap(following, "x", 1), lax.ppermute(following, ROW, odd), swap(following, "x", 2), far)
    line = jnp.stack([v[:, :C] for v in (following,) + near])
    sums = after(sum(v[:, C:] for v in near[:3]) + following[:, C:], near[3])
    carried = jnp.concatenate([line.reshape(5 * K, C), jnp.pad(sums, ((0, 0), (0, C - W)))], axis=0)
    core = swap(carried, "c", 1)
    side = over_side(line)
    sums = sums + core[5 * K :, :W]
    near, second = call(second_kernel, (like(spheres, C), like(spheres, C)), 10, work=5 * 10**9)(
        line, core, side, matrix, *weights, mie, member, first
    )
    sums = plus(sums, "z", (2, 6, 4))
    sums = plus(sums, "y", (2, 1, 3))
    entries = float(lax.axis_size(ALL) * spheres * C)
    return tuple(
        call(functools.partial(last_kernel, entries), (like(spheres, C), like(spheres, C)), 4)(
            kept, near, second, sums
        )
    )


def solution(mesh):
    torus = Mesh(mesh.devices.reshape(4, 2, 8, 4), ALL)
    return jax.shard_map(
        body,
        mesh=torus,
        in_specs=(
            P(ALL, None),
            P(ALL),
            P(ALL, None),
            P(ALL),
            P(ALL),
            P(ALL),
            P(ALL, None, None),
            P(),
            P(),
            P(),
        ),
        out_specs=(P(ALL, None), P(ALL, None)),
        check_vma=False,
    )
```

```python
import functools

import jax
import jax.numpy as jnp
from jax import lax
from jax.experimental import pallas as pl
from jax.experimental.pallas import tpu as pltpu
from jax.sharding import Mesh
from jax.sharding import PartitionSpec as P

F32 = jnp.float32
BF16 = jnp.bfloat16
ALL = ("y", "c", "z", "x")
ROW = ("z", "x")
COL = ("y", "c")
K = 8
C = 1920
NB = 15
W = 128
NPEER = 14
CAP = 4
EXTRA = 256
VMEM_LIMIT = 24 * 1024 * 1024

NN = (((1,), (0,)), ((), ()))
NT = (((1,), (1,)), ((), ()))
TN = (((0,), (0,)), ((), ()))


def halves(x):
    high = x.astype(BF16)
    return high, (x - high.astype(F32)).astype(BF16)


def dot3(a, b, dims=NN):
    rows = a.shape[0]
    a_high32 = a.astype(BF16).astype(F32)
    both = jnp.concatenate([a_high32, a - a_high32], axis=0).astype(BF16)
    b_high, b_low = halves(b)
    first = lax.dot_general(both, b_high, dims, preferred_element_type=F32)
    second = lax.dot_general(a.astype(BF16), b_low, dims, preferred_element_type=F32)
    return first[:rows] + first[rows:] + second


def thirds(x):
    high = x.astype(BF16).astype(F32)
    rest = x - high
    middle = rest.astype(BF16).astype(F32)
    return high, middle, rest - middle


def weighted_hot(x, hot):
    rows = x.shape[0]
    out = lax.dot_general(
        jnp.concatenate(thirds(x), axis=0).astype(BF16), hot.astype(BF16), NT, preferred_element_type=F32
    )
    return out[:rows] + out[rows : 2 * rows] + out[2 * rows :]


def hot_times(hot, x, dims=NN):
    hot = hot.astype(BF16)
    return sum(lax.dot_general(hot, part.astype(BF16), dims, preferred_element_type=F32) for part in thirds(x))


def rows_of(member, x):
    return lax.dot_general(
        jnp.concatenate([member] * 3, axis=0).astype(BF16),
        jnp.concatenate(thirds(x), axis=0).astype(BF16),
        TN,
        preferred_element_type=F32,
    )


def lanes(shape):
    return lax.broadcasted_iota(jnp.int32, shape, 1)


def sublanes(shape):
    return lax.broadcasted_iota(jnp.int32, shape, 0)


def gather_kernel(count_ref, *refs):
    sources, (out_ref, square_ref, rhs_ref), (pad_ref, member_ref, ends_ref, dir_ref, reach_ref, send_ref, sem) = (
        refs[:6],
        refs[6:9],
        refs[9:],
    )
    targets = (rhs_ref, member_ref, ends_ref, dir_ref, reach_ref, send_ref)
    copies = [pltpu.make_async_copy(a, b, sem.at[i]) for i, (a, b) in enumerate(zip(sources, targets))]
    for copy in copies:
        copy.start()
    for copy in copies:
        copy.wait()
    spheres = rhs_ref.shape[0]
    pairs = dir_ref.shape[1]
    rhs = rhs_ref[...]
    member = (sublanes((K, spheres)) == member_ref[...]).astype(F32)
    out_ref[:, :C] = hot_times(member, rhs)
    squares = jnp.sum(rhs * rhs, axis=0, keepdims=True)
    partial = squares[:, :W]
    for g in range(1, NB):
        partial = partial + squares[:, g * W : (g + 1) * W]
    square_ref[...] = partial
    weight = jnp.where(lanes((1, pairs)) < count_ref[0], reach_ref[...], 0.0)
    own = ends_ref[0:1, :]
    near = ends_ref[1:2, :]
    far = near - K
    place = jnp.where(near < K, near, K + NPEER * (far & (CAP - 1)) + (far >> 2))
    rows = sublanes((W, pairs)) & 63
    near_hot = (rows == place).astype(F32)
    own_weight = jnp.where(sublanes((K, pairs)) == own, weight, 0.0)
    lane = lanes((K, W))
    classes = jnp.concatenate([jnp.where(dir_ref[...] == d, own_weight, 0.0) for d in range(3)], axis=0)
    table = weighted_hot(classes, near_hot)
    blocks = [table[d * K : d * K + K] for d in range(3)]
    pad_ref[...] = jnp.zeros_like(pad_ref)
    pad_ref[0:CAP, 0:NPEER] = send_ref[...].astype(F32)
    names = jnp.where(lane < 64 + K, (lane - 64).astype(F32), 0.0)
    for slot in range(CAP):
        row = jnp.broadcast_to(pad_ref[slot : slot + 1, :], (K, W))
        names = names + pltpu.roll(row, 64 + K + NPEER * slot, 1)
    out_ref[:, C : C + W] = jnp.where(lane < 64, blocks[0], blocks[1])
    out_ref[:, C + W :] = jnp.where(lane < 64, blocks[2], names)


def pair_matrix(units):
    x = lax.axis_index("x")
    c = lax.axis_index("c")
    core = 1 - 2 * c
    one = 1 - 2 * (x & 1)
    two = jnp.where(x < 2, 2, -2)
    lane = lanes((K, W))
    low = lane < 64
    half = lane & 63
    seen = half - K
    peer = seen - NPEER * (
        (seen >= NPEER).astype(jnp.int32)
        + (seen >= 2 * NPEER).astype(jnp.int32)
        + (seen >= 3 * NPEER).astype(jnp.int32)
    )
    peer = jnp.where(half < K, -1, peer)
    names_of = sublanes((K, W)).astype(F32)
    hot, first, second = [], [], []
    for group, d_row in enumerate((0, core, -core)):
        for place, d_col in enumerate((0, one, -one, two, -two)):
            v0, v1 = units[group * 5 + place]
            names = jnp.where(low, pltpu.roll(v1, 64, 1), v1)
            if group == 0 and place == 0:
                here = peer == -1
                there = here
                own_hot = jnp.where(names == names_of, 1.0, 0.0)
            else:
                f = (1 - d_row) * 5 + 2 - d_col
                b = 14 - f
                here = peer == f - (f > 7).astype(jnp.int32)
                there = peer == b - (b > 7).astype(jnp.int32)
            hot.append(jnp.where((names == names_of) & here, 1.0, 0.0))
            first.append(jnp.where(there, v0, 0.0))
            second.append(jnp.where(there & low, v1, 0.0))
    hot = jnp.concatenate(hot, axis=0)
    first = jnp.concatenate(first, axis=0)
    second = jnp.concatenate(second, axis=0)
    v0, v1 = units[0]

    def two_classes(v):
        return jnp.concatenate([jnp.where(low, v, 0.0), jnp.where(low, 0.0, v)], axis=0)

    ends = jnp.concatenate([two_classes(v0), jnp.where(low, v1, 0.0)], axis=0)
    return jnp.concatenate(
        [
            weighted_hot(ends, hot),
            hot_times(two_classes(own_hot), first, NT),
            hot_times(jnp.where(low, own_hot, 0.0), second, NT),
        ],
        axis=0,
    )


def stacked(x):
    high = x.astype(BF16).astype(F32)
    return jnp.concatenate([high, x - high], axis=0).astype(BF16)


def times(x, parts):
    rows, columns = x.shape[0], parts.shape[1] // 2
    out = lax.dot_general(stacked(x), parts, NN, preferred_element_type=F32)
    return out[:rows, :columns] + (out[:rows, columns:] + out[rows:, :columns]) + out[rows:, columns:]


def split_kernel(rotation_any, translation_any, turn_ref, move_ref, back_ref, rotation_ref, translation_ref, sem):
    copies = start_all((rotation_any, translation_any), (rotation_ref, translation_ref), sem)

    def put(ref, g, row, w):
        ref[g, row : row + W, :] = jnp.concatenate(halves(w), axis=1)

    copies[0].wait()
    for g in range(NB):
        for d in range(3):
            w = rotation_ref[d, g]
            put(turn_ref, g, d * W, w)
            put(back_ref, g, d * W, w.T)
    copies[1].wait()
    for g in range(NB):
        w = translation_ref[g]
        put(move_ref, g, 0, w)
        put(move_ref, g, W, w.T)


def field_of(matrix, rows, turn_ref, move_ref, back_ref):
    ends = dot3(matrix, rows)
    low = lanes((3 * K, W)) < 64
    turned = []
    for g in range(NB):
        at = slice(g * W, (g + 1) * W)
        parts = []
        for d in range(3):
            pair = jnp.concatenate([ends[d * K : d * K + K, at], ends[24 + d * K : 24 + d * K + K, at]], axis=0)
            parts.append(pltpu.roll(times(pair, turn_ref[g, d * W : (d + 1) * W, :]), 64, 1))
        front = jnp.concatenate([p[:K] for p in parts], axis=0)
        behind = jnp.concatenate([p[K:] for p in parts], axis=0)
        turned.append((front, behind))
    moved = []
    for g in range(NB):
        both = [jnp.where(low, before, here) for before, here in zip(turned[g - 1], turned[g])]
        moved.append(pltpu.roll(times(jnp.concatenate(both, axis=1), move_ref[g]), 64, 1))
    out = []
    for g in range(NB):
        z = jnp.where(low, moved[g], moved[(g + 1) % NB])
        flat = jnp.concatenate([z[d * K : d * K + K] for d in range(3)], axis=1)
        out.append(times(flat, back_ref[g]))
    return out


def start_all(sources, targets, sem):
    copies = [pltpu.make_async_copy(a, b, sem.at[i]) for i, (a, b) in enumerate(zip(sources, targets))]
    for copy in copies:
        copy.start()
    return copies


def first_kernel(
    own_ref, core_ref, side_ref, square_ref, turn_ref, move_ref, back_ref, mie_ref, member_ref,
    matrix_ref, field_ref, next_ref, sums_ref,
):
    refs = [r.at[i] for r in (own_ref, core_ref, side_ref) for i in range(5)]
    matrix = pair_matrix([(r[:, C : C + W], r[:, C + W : C + 2 * W]) for r in refs])
    matrix_ref[...] = matrix
    rows = jnp.concatenate([r[:, :C] for r in refs], axis=0)
    field = field_of(matrix, rows, turn_ref, move_ref, back_ref)
    spheres = member_ref.shape[1]
    member = (sublanes((K, spheres)) == member_ref[...]).astype(F32)
    count = jnp.sum(member, axis=1, keepdims=True)
    inner = jnp.zeros((K, W), F32)
    square = jnp.zeros((K, W), F32)
    for g in range(NB):
        at = slice(g * W, (g + 1) * W)
        scaled = field[g] * mie_ref[g : g + 1, :]
        total = scaled * count
        field_ref[:, at] = scaled
        next_ref[:, at] = total
        inner = inner + scaled * own_ref[0, :, at]
        square = square + scaled * total
    row = sublanes((K, W))
    inner = jnp.sum(inner, axis=0, keepdims=True)
    square = jnp.sum(square, axis=0, keepdims=True)
    sums_ref[...] = jnp.where(row == 0, square_ref[...], jnp.where(row == 1, inner, jnp.where(row == 2, square, 0.0)))


def second_kernel(
    own_ref, core_ref, side_ref, matrix_ref, turn_ref, move_ref, back_ref, mie_ref, member_ref, first_ref,
    near_ref, next_ref,
):
    core = [core_ref[i * K : i * K + K, :] for i in range(5)]
    rows = jnp.concatenate([own_ref[i] for i in range(5)] + core + [side_ref[i] for i in range(5)], axis=0)
    field = field_of(matrix_ref[...], rows, turn_ref, move_ref, back_ref)
    spheres = member_ref.shape[1]
    member = (sublanes((K, spheres)) == member_ref[...]).astype(F32)
    for g in range(NB):
        at = slice(g * W, (g + 1) * W)
        near_ref[:, at] = rows_of(member, first_ref[:, at])
        next_ref[:, at] = rows_of(member, field[g] * mie_ref[g : g + 1, :])


def last_kernel(entries, rhs_ref, first_ref, second_ref, sums_ref, basis_ref, image_ref):
    sums = jnp.sum(sums_ref[...], axis=1, keepdims=True) / entries
    s, t, u = sums[0:1], sums[1:2], sums[2:3]
    scale2 = s + 1e-06
    rest = (1e-06 + t) / scale2
    norm = jnp.sqrt((rest * rest * s - 2.0 * rest * t + u) / scale2 + 1e-06)
    factor = 1.0 / (norm * jnp.sqrt(scale2))
    first = first_ref[...] * factor
    basis = (rest * factor) * rhs_ref[...] - first
    basis_ref[...] = basis
    image_ref[...] = basis - (rest * first - second_ref[...] * factor)


def call(kernel, out_shape, vmem, anywhere=0, scratch=(), smem=0, work=0):
    space = [pl.BlockSpec(memory_space=pltpu.SMEM)] * smem + [pl.BlockSpec(memory_space=pltpu.VMEM)] * vmem
    space += [pl.BlockSpec(memory_space=pltpu.HBM)] * anywhere
    run = pl.pallas_call(
        kernel,
        out_shape=out_shape,
        in_specs=space,
        scratch_shapes=list(scratch),
        compiler_params=pltpu.CompilerParams(vmem_limit_bytes=VMEM_LIMIT),
        cost_estimate=pl.CostEstimate(flops=work, bytes_accessed=0, transcendentals=0) if work else None,
    )

    def placed(*operands):
        held = [pltpu.with_memory_space_constraint(v, pltpu.HBM) for v in operands[smem + vmem :]]
        return run(*operands[: smem + vmem], *held)

    return placed


def like(*shape):
    return jax.ShapeDtypeStruct(shape, F32)


def swap(v, axis, mask):
    return lax.ppermute(v, axis, [(i, i ^ mask) for i in range(lax.axis_size(axis))])


def row_pairs():
    length = lax.axis_size("z")
    devices = 4 * length
    inside = [(4 * z + 1, 4 * z + 2) for z in range(length)]
    odd = inside + [(4 * z + 3, (4 * z + 4) % devices) for z in range(length)]
    wide = [(4 * z + i, (4 * z + i + 2) % devices) for z in range(length) for i in (2, 3)]
    return [odd + [(b, a) for a, b in odd], wide + [(b, a) for a, b in wide]]


def beside(v):
    odd, wide = row_pairs()
    return swap(v, "x", 1), lax.ppermute(v, ROW, odd), swap(v, "x", 2), lax.ppermute(v, ROW, wide)


def over_side(line):
    devices = lax.axis_size(COL)
    steps = [(i, (i + 1) % devices) for i in range(1, devices, 2)]
    return lax.ppermute(line, COL, steps + [(b, a) for a, b in steps])


def after(v, other):
    return lax.optimization_barrier((v, other))[0]


def plus(v, axis, masks):
    return functools.reduce(jnp.add, [v] + [swap(v, axis, mask) for mask in masks])


def body(rhs, membership, pair_ends, pair_dir, pair_reach, pair_count, send_idx, rotation, translation, mie):
    spheres = rhs.shape[0]
    pairs = pair_dir.shape[0]
    member = membership.reshape(1, spheres)
    mie = mie.reshape(NB, W)
    whole = [
        pltpu.VMEM((1, spheres), jnp.int32),
        pltpu.VMEM((2, pairs), jnp.int32),
        pltpu.VMEM((1, pairs), jnp.int32),
        pltpu.VMEM((1, pairs), F32),
        pltpu.VMEM((CAP, NPEER), jnp.int32),
        pltpu.SemaphoreType.DMA((6,)),
    ]
    packed, squares, kept = call(
        gather_kernel,
        (like(K, C + EXTRA), like(1, W), like(spheres, C)),
        0,
        6,
        [pltpu.VMEM((K, W), F32)] + whole,
        1,
    )(
        pair_count,
        rhs,
        member,
        pair_ends.T,
        pair_dir.reshape(1, pairs),
        pair_reach.reshape(1, pairs),
        jnp.transpose(send_idx, (0, 2, 1)).reshape(CAP, NPEER),
    )
    weights = call(
        split_kernel,
        tuple(jax.ShapeDtypeStruct((NB, rows * W, 2 * W), BF16) for rows in (3, 2, 3)),
        0,
        2,
        [pltpu.VMEM(rotation.shape, F32), pltpu.VMEM(translation.shape, F32), pltpu.SemaphoreType.DMA((2,))],
        work=3 * 10**9,
    )(rotation, translation)
    line = jnp.stack((packed,) + beside(packed))
    matrix, first, following, sums = call(
        first_kernel, (like(6 * K, 15 * K), like(K, C), like(K, C), like(K, W)), 9
    )(
        line, swap(line, "c", 1), over_side(line), squares, *weights, mie, member
    )
    odd, wide = row_pairs()
    far = lax.ppermute(following, ROW, wide)
    following = jnp.concatenate([following, plus(sums, "z", (1,))], axis=1)
    near = (swap(following, "x", 1), lax.ppermute(following, ROW, odd), swap(following, "x", 2), far)
    line = jnp.stack([v[:, :C] for v in (following,) + near])
    sums = after(sum(v[:, C:] for v in near[:3]) + following[:, C:], near[3])
    carried = jnp.concatenate([line.reshape(5 * K, C), jnp.pad(sums, ((0, 0), (0, C - W)))], axis=0)
    core = swap(carried, "c", 1)
    side = over_side(line)
    sums = sums + core[5 * K :, :W]
    near, second = call(second_kernel, (like(spheres, C), like(spheres, C)), 10, work=5 * 10**9)(
        line, core, side, matrix, *weights, mie, member, first
    )
    sums = plus(sums, "z", (2, 6, 4))
    sums = plus(sums, "y", (1, 3, 2))
    entries = float(lax.axis_size(ALL) * spheres * C)
    return tuple(
        call(functools.partial(last_kernel, entries), (like(spheres, C), like(spheres, C)), 4)(
            kept, near, second, sums
        )
    )


def solution(mesh):
    torus = Mesh(mesh.devices.reshape(4, 2, 8, 4), ALL)
    return jax.shard_map(
        body,
        mesh=torus,
        in_specs=(
            P(ALL, None),
            P(ALL),
            P(ALL, None),
            P(ALL),
            P(ALL),
            P(ALL),
            P(ALL, None, None),
            P(),
            P(),
            P(),
        ),
        out_specs=(P(ALL, None), P(ALL, None)),
        check_vma=False,
    )
```
